256 devices in a mesh: dp: 16 (over z_hi, x, core), expert: 16 (over z_lo, y).
Axes of the slice: x: 4, y: 4, z: 8 (z_hi: 2, z_lo: 4; z = z_hi * 4 + z_lo), core: 2. Of those that a mesh axis runs over, the one named last changes fastest.
Arguments:
- patches: bfloat16 [32, 256, 2048], P('dp', None, 'expert'), may hold values from -6 to 6
- visible: int32 [32, 64], P('dp'), may hold values from 0 to 255, as said below
- modality: int32 [32, 64], P('dp'), may hold values from 0 to 1, as said below
- dropped: int32 [32], P('dp'), may hold values from 0 to 2
- attn_gain: float32 [2048], replicated, may hold values from 0.1 to 1.9
- w_qkv: bfloat16 [2048, 3, 2048], P(None, None, 'expert')
- w_out: bfloat16 [2048, 2048], P('expert'), may hold values from -0.125 to 0.125
- ffn_gain: float32 [2048], replicated, may hold values from 0.1 to 1.9
- w_gate: bfloat16 [16, 2048, 4096], P('expert', None, 'dp'), as said below
- w_up: bfloat16 [16, 2048, 4096], P('expert', None, 'dp'), as said below
- w_down: bfloat16 [16, 4096, 2048], P('expert', 'dp'), as said below
- cotangent: bfloat16 [2048, 2048], P(('dp', 'expert')), may hold values from -6 to 6
Outputs:
- output: bfloat16 [2048, 2048], P(('dp', 'expert'))
- grad_qkv: float32 [2048, 3, 2048], P(None, None, 'expert')
- grad_out: float32 [2048, 2048], P('expert')
The draws below stay inside these ranges and needn't reach their ends.
Inputs may be any that keep to these rules, and one draw needn't show every extreme that they name: `visible`: the 64 indices of each sample are distinct. `modality`: each sample has exactly 16 tokens of value 1. w_gate[e] equals w_gate[e % 2] for e < 12 and w_gate[12 + (e - 12) % 2] otherwise. w_up[e] equals w_up[e % 2] for e < 12 and w_up[12 + (e - 12) % 2] otherwise. w_down[e] equals w_down[e % 2] for e < 12 and w_down[12 + (e - 12) % 2] otherwise.
All inputs are finite; a program needn't handle non-finite values.
Results may differ from the reference program's by a relative error of at most 0.03.
The reference program's roundings to bfloat16 on the way count: a program that leaves them out, or rounds other values in their place, can miss the bound.
Values may be sent and summed in bfloat16 or wider, within the bound.
A program may use at most 64 MiB of HBM per device.

```python
import math
import jax
import jax.numpy as jnp
from jax import lax

D = 2048
HEADS = 16
HEAD_DIM = 128
FF = 8192
VIS = 64
PATCHES = 256
SAMPLES = 32
TOKENS = 2048
SPLIT = 2
OPT_COLS = 12
FF_DEV = 256
N_EXPERT = 16


def replicated_blocks(key, row_size, col_size, fan_in):
    split_count = N_EXPERT // 8
    opt_count = 3 * N_EXPERT // 4
    base = jax.random.normal(key, (2 * split_count, row_size, col_size), jnp.float32) / math.sqrt(fan_in)
    column_ids = jnp.arange(N_EXPERT, dtype=jnp.int32)
    pick_ids = jnp.where(column_ids < opt_count, column_ids % split_count, split_count + (column_ids - opt_count) % split_count)
    return jnp.take(base, pick_ids, axis=0).astype(jnp.bfloat16)


def draw_w_gate(key, part):
    key = jax.random.fold_in(key, 11)
    return replicated_blocks(key, D, FF // (N_EXPERT // 8), D)


def draw_w_up(key, part):
    key = jax.random.fold_in(key, 12)
    return replicated_blocks(key, D, FF // (N_EXPERT // 8), D)


def draw_w_down(key, part):
    key = jax.random.fold_in(key, 13)
    return replicated_blocks(key, FF // (N_EXPERT // 8), D, FF)


def draw_w_qkv(key, part):
    key = jax.random.fold_in(key, 5)
    draws = jax.random.normal(key, (D, 3, D), jnp.float32) / math.sqrt(D)
    return draws.astype(jnp.bfloat16)


def draw_visible(key, part):
    key = jax.random.fold_in(key, 7)
    sample_keys = jax.random.split(key, SAMPLES)
    chosen = jax.vmap(lambda sample_key: jax.random.permutation(sample_key, PATCHES)[:VIS])(sample_keys)
    return chosen.astype(jnp.int32)


def draw_modality(key, part):
    key = jax.random.fold_in(key, 9)
    sample_keys = jax.random.split(key, SAMPLES)
    shuffled = jax.vmap(lambda sample_key: jax.random.permutation(sample_key, VIS))(sample_keys)
    return (shuffled < VIS // 4).astype(jnp.int32)


def plant(array, rng, smallest, top_value):
    longest = array.shape.index(max(array.shape))
    spots = []
    for shift in (0, 1):
        where = [jax.random.randint(jax.random.fold_in(rng, axis), (), 0, length) for axis, length in enumerate(array.shape)]
        where[longest] = (where[longest] + shift) % array.shape[longest]
        spots.append(tuple(where))
    return array.at[spots[0]].set(smallest).at[spots[1]].set(top_value)


def block_scale(rng, dims, cuts, low, top_value):
    level = 1.0
    for position, shards_of in cuts:
        heights = jax.random.uniform(jax.random.fold_in(jax.random.fold_in(rng, 6), position), (shards_of,), jnp.float32, low / len(cuts), top_value / len(cuts))
        level = level * jnp.repeat(jnp.exp(heights), dims[position] // shards_of).reshape((-1,) + (1,) * (len(dims) - 1 - position))
    return level


def bell_draw(rng, shape, deviation, most, shards=(), held_as=jnp.bfloat16):
    result = jax.random.normal(rng, shape, jnp.float32) * deviation
    if len(shards) > 0:
        result = block_scale(rng, shape, shards, -0.22, 0.18) * result
    return jnp.clip(result, min=-most, max=most).astype(held_as)


def setup_inputs(seed: int = 0) -> dict:
    key_of = jax.random.split(jax.random.key(seed), 13)
    return {
        "patches": bell_draw(key_of[0], (SAMPLES, PATCHES, D), 1.0, 6.0, ((0, 16), (2, 16))),
        "visible": draw_visible(jax.random.fold_in(key_of[12], 71), 0),
        "modality": draw_modality(jax.random.fold_in(key_of[12], 71), 0),
        "dropped": plant(jax.random.randint(key_of[3], (SAMPLES,), 0, 3), jax.random.fold_in(key_of[3], 1), 0, 2).astype(jnp.int32),
        "attn_gain": jnp.clip(1.0 + 0.18 * jax.random.normal(key_of[4], (D,), jnp.float32), 0.1, 1.9),
        "w_qkv": draw_w_qkv(jax.random.fold_in(key_of[12], 71), 0),
        "w_out": bell_draw(key_of[6], (D, D), D ** -0.5, 0.125, ((0, 16),)),
        "ffn_gain": jnp.clip(1.0 + 0.18 * jax.random.normal(key_of[7], (D,), jnp.float32), 0.1, 1.9),
        "w_gate": draw_w_gate(jax.random.fold_in(key_of[12], 71), 0),
        "w_up": draw_w_up(jax.random.fold_in(key_of[12], 71), 0),
        "w_down": draw_w_down(jax.random.fold_in(key_of[12], 71), 0),
        "cotangent": bell_draw(key_of[11], (TOKENS, D), 1.0, 6.0, ((0, 256),)),
    }


def rms_scale(values, gain):
    mean_sq = lax.optimization_barrier(jnp.mean(values * values, axis=-1, keepdims=True))
    return values * lax.rsqrt(mean_sq + 1e-06) * gain

def attend(queries, key_heads, value_heads, alive_grid):
    factor = 1.0 / math.sqrt(queries.shape[-1])
    scores = jnp.einsum('shqe,shke->shqk', queries.astype(jnp.float32), key_heads.astype(jnp.float32)) * factor
    scores = jnp.where(alive_grid[:, None, None, :], scores, -1e+30)
    row_top = lax.stop_gradient(lax.optimization_barrier(jnp.max(scores, axis=-1, keepdims=True)))
    weights = jnp.exp(scores - row_top)
    probs = (weights / lax.optimization_barrier(jnp.sum(weights, axis=-1, keepdims=True))).astype(jnp.bfloat16)
    return jnp.einsum('shqk,shke->shqe', probs.astype(jnp.float32), value_heads.astype(jnp.float32))

def settle(values):
    return lax.optimization_barrier(values.astype(jnp.bfloat16)).astype(jnp.float32)

def block_terms(tok_in, grad_in, gate_part, up_part, down_part):
    gate_acts = jnp.dot(tok_in, gate_part, preferred_element_type=jnp.float32)
    up_acts = jnp.dot(tok_in, up_part, preferred_element_type=jnp.float32)
    logistic = jax.nn.sigmoid(gate_acts)
    active = gate_acts * logistic
    hidden = (active * up_acts).astype(jnp.bfloat16)
    out_part = jnp.dot(hidden, down_part, preferred_element_type=jnp.float32)
    grad_hidden = jnp.dot(grad_in, down_part.T, preferred_element_type=jnp.float32)
    grad_gate = (grad_hidden * up_acts * logistic * (1.0 + gate_acts * (1.0 - logistic))).astype(jnp.bfloat16)
    grad_up = (grad_hidden * active).astype(jnp.bfloat16)
    back_part = jnp.dot(grad_gate, gate_part.T, preferred_element_type=jnp.float32) + jnp.dot(grad_up, up_part.T, preferred_element_type=jnp.float32)
    return (out_part, back_part)

def reference(patches, visible, modality, dropped, attn_gain, w_qkv, w_out, ffn_gain, w_gate, w_up, w_down, cotangent):
    picked = jnp.take_along_axis(patches, visible[:, :, None].astype(jnp.int32), axis=1)
    tok_rows = picked.reshape(TOKENS, D)
    alive_grid = jnp.logical_or(dropped[:, None] == 0, modality != dropped[:, None] - 1)
    normed = rms_scale(tok_rows.astype(jnp.float32), attn_gain).astype(jnp.bfloat16)
    projected = jnp.dot(normed, w_qkv.reshape(D, 3 * D), preferred_element_type=jnp.float32).astype(jnp.bfloat16)
    projected = projected.reshape(SAMPLES, VIS, 3, HEADS, HEAD_DIM)
    queries = projected[:, :, 0].transpose(0, 2, 1, 3)
    key_heads = projected[:, :, 1].transpose(0, 2, 1, 3)
    value_heads = projected[:, :, 2].transpose(0, 2, 1, 3)
    attended, pullback = jax.vjp(lambda q_part, k_part, v_part: attend(q_part, k_part, v_part, alive_grid), queries, key_heads, value_heads)
    head_out = attended.astype(jnp.bfloat16).transpose(0, 2, 1, 3).reshape(TOKENS, D)
    residual = tok_rows.astype(jnp.float32) + jnp.dot(head_out, w_out, preferred_element_type=jnp.float32)
    normed_res, norm_back = jax.vjp(lambda values: rms_scale(values, ffn_gain), residual)
    token_bf = normed_res.astype(jnp.bfloat16)
    kind_rows = modality.reshape(TOKENS).astype(jnp.int32)
    live_rows = alive_grid.reshape(TOKENS)
    order_idx = jnp.argsort(kind_rows, stable=True).astype(jnp.int32)
    inverse_idx = jnp.argsort(order_idx).astype(jnp.int32)
    sorted_tok = jnp.where(live_rows[order_idx][:, None], token_bf[order_idx], jnp.zeros_like(token_bf))
    sorted_grad = jnp.where(live_rows[order_idx][:, None], cotangent[order_idx], jnp.zeros_like(cotangent))
    opt_rows = 3 * TOKENS // 4
    out_pieces = []
    back_pieces = []
    for first_col, row_from, row_to in ((0, 0, opt_rows), (OPT_COLS, opt_rows, TOKENS)):
        gate_full = jnp.concatenate([w_gate[first_col + piece_idx] for piece_idx in range(SPLIT)], axis=1)
        up_full = jnp.concatenate([w_up[first_col + piece_idx] for piece_idx in range(SPLIT)], axis=1)
        down_full = jnp.concatenate([w_down[first_col + piece_idx] for piece_idx in range(SPLIT)], axis=0)
        tok_in = sorted_tok[row_from:row_to]
        grad_in = sorted_grad[row_from:row_to]
        out_total = jnp.zeros((row_to - row_from, D), jnp.float32)
        back_total = jnp.zeros((row_to - row_from, D), jnp.float32)
        for block_idx in range(FF // FF_DEV):
            lower = block_idx * FF_DEV
            upper = lower + FF_DEV
            out_part, back_part = block_terms(tok_in, grad_in, gate_full[:, lower:upper], up_full[:, lower:upper], down_full[lower:upper])
            out_total = out_total + settle(out_part)
            back_total = back_total + settle(back_part)
        out_pieces.append(out_total)
        back_pieces.append(back_total)
    expert_out = jnp.concatenate(out_pieces, axis=0)[inverse_idx]
    grad_in_all = jnp.concatenate(back_pieces, axis=0)[inverse_idx]
    output = (residual + expert_out).astype(jnp.bfloat16)
    grad_resid = (cotangent.astype(jnp.float32) + norm_back(grad_in_all)[0]).astype(jnp.bfloat16)
    grad_out = jnp.dot(head_out.T, grad_resid, preferred_element_type=jnp.float32)
    grad_attended = jnp.dot(grad_resid, w_out.T, preferred_element_type=jnp.float32)
    grad_attended = grad_attended.reshape(SAMPLES, VIS, HEADS, HEAD_DIM).transpose(0, 2, 1, 3)
    grad_query, grad_keys, grad_values = pullback(grad_attended)
    stacked = jnp.stack([grad_part.transpose(0, 2, 1, 3) for grad_part in (grad_query, grad_keys, grad_values)], axis=2)
    stacked = stacked.reshape(TOKENS, 3 * D)
    grad_qkv = jnp.dot(normed.T, stacked, preferred_element_type=jnp.float32).reshape(D, 3, D)
    return (output, grad_qkv, grad_out)
```

```python
import math

import jax
import jax.numpy as jnp
from jax import lax
from jax.experimental import pallas as pl
from jax.experimental.pallas import tpu as pltpu
from jax.sharding import PartitionSpec as P

BF = jnp.bfloat16
F32 = jnp.float32
MESH = pl.DeviceIdType.MESH
D = 2048
EPS = 1e-06
FACTOR = 1.0 / math.sqrt(128)


def dot(a, b):
    return jnp.dot(a, b, preferred_element_type=F32)


def dot_nt(a, b):
    return lax.dot_general(a, b, (((1,), (1,)), ((), ())), preferred_element_type=F32)


def kernel(
    dropped_ref,
    patches_ref,
    visible_ref,
    modality_ref,
    again_ref,
    fgain_ref,
    cot_ref,
    wqkv_hbm,
    wout_hbm,
    wg_hbm,
    wu_hbm,
    wd_hbm,
    out_ref,
    gfin,
    wqkv,
    wout,
    wg,
    wu,
    wd,
    gath,
    cotg,
    part,
    attr,
    normed,
    norm_t,
    probs32,
    tokg,
    cotr,
    tmat,
    cmat,
    osum,
    r1,
    s1,
    r2,
    s3,
    r3,
    outg,
    grg,
    grmat,
    gbuf,
    h1,
    t1,
    h2,
    t3,
    h3,
    wsem,
    ssem,
    sem_pick,
    sem_cot,
    sem_attn,
    sem_tok,
    sem_cotr,
    sem_d1,
    sem_d2,
    sem_d3,
    sem_gr,
    sem_out,
    sem_g1,
    sem_g2,
    sem_g3,
    sem_fin,
):
    d = lax.axis_index("dp")
    e = lax.axis_index("expert")
    zh = d // 8
    x = (d // 2) % 4
    c = d % 2
    zl = e // 4
    y = e % 4
    h = y % 2
    xh = x * 2 + h
    sib = (zh * 8 + x * 2 + (1 - c), e)
    z_row = (1 - zh) * 8 + x * 2 + c
    zpart = (z_row, ((6 - zl) % 4) * 4 + y)
    zsame = (z_row, e)

    def exp_peer(k):
        q = (e + k) % 16
        return q, (d, q)

    def xh_peer(k):
        q = (xh + k) % 8
        return q, (zh * 8 + (q // 2) * 2 + c, zl * 4 + (y // 2) * 2 + q % 2)

    def x_peer(k):
        q = (x + k) % 4
        return q, (zh * 8 + q * 2 + c, e)

    def send(src, dst, s_sem, r_sem, dev):
        pltpu.make_async_remote_copy(
            src_ref=src, dst_ref=dst, send_sem=s_sem, recv_sem=r_sem,
            device_id=dev, device_id_type=MESH,
        ).start()

    def arrived(dst, r_sem):
        pltpu.make_async_remote_copy(
            src_ref=dst, dst_ref=dst, send_sem=ssem.at[0], recv_sem=r_sem,
            device_id=sib, device_id_type=MESH,
        ).wait_recv()

    def sent(src, s_sem):
        pltpu.make_async_remote_copy(
            src_ref=src, dst_ref=src, send_sem=s_sem, recv_sem=sem_d3.at[0],
            device_id=sib, device_id_type=MESH,
        ).wait_send()

    def loop(lo, hi, fn):
        def step(k, carry):
            fn(k)
            return carry

        lax.fori_loop(lo, hi, step, 0)

    loads = [
        pltpu.make_async_copy(src, dst, wsem.at[i])
        for i, (src, dst) in enumerate(
            ((wqkv_hbm, wqkv), (wout_hbm, wout), (wg_hbm, wg), (wu_hbm, wu), (wd_hbm, wd))
        )
    ]
    for load in loads:
        load.start()

    barrier = pltpu.get_barrier_semaphore()

    def greet(dev):
        pl.semaphore_signal(barrier, inc=1, device_id=dev, device_id_type=MESH)

    loop(1, 16, lambda k: greet(exp_peer(k)[1]))
    loop(1, 8, lambda k: greet(xh_peer(k)[1]))
    greet(sib)
    greet(zpart)
    greet(zsame)

    mod = modality_ref[...].astype(F32)
    upto = (
        lax.broadcasted_iota(jnp.int32, (64, 64), 0) <= lax.broadcasted_iota(jnp.int32, (64, 64), 1)
    ).astype(F32)
    samp_col = lax.broadcasted_iota(jnp.int32, (2, 64), 0).astype(F32)
    rank_sar = dot(mod, upto) - 1.0
    rank_opt = dot(1.0 - mod, upto) - 1.0
    place = jnp.where(mod > 0.5, 96.0 + 16.0 * samp_col + rank_sar, 48.0 * samp_col + rank_opt)
    slot_iota = lax.broadcasted_iota(jnp.int32, (128, 64), 0).astype(F32)
    patch_iota = lax.broadcasted_iota(jnp.int32, (256, 64), 0)
    place_hot = [
        jnp.where(slot_iota == place[s : s + 1, :], 1.0, 0.0).astype(BF) for s in range(2)
    ]
    picked = jnp.zeros((128, 128), F32)
    for s in range(2):
        patch_hot = jnp.where(patch_iota == visible_ref[s : s + 1, :], 1.0, 0.0).astype(BF)
        picked += dot(dot_nt(place_hot[s], patch_hot).astype(BF), patches_ref[s])
    gath[e] = picked.reshape(16, 8, 128).astype(BF)
    cotg[e] = cot_ref[...]

    pl.semaphore_wait(barrier, 25)

    def send_pick(k):
        q, dev = exp_peer(k)
        send(gath.at[e], gath.at[e], ssem.at[0], sem_pick.at[e], dev)

    loop(1, 16, send_pick)

    def send_cot(k):
        q, dev = exp_peer(k)
        send(cotg.at[e], cotg.at[e], ssem.at[1], sem_cot.at[e], dev)

    loop(1, 16, send_cot)

    def wait_pick(k):
        q, dev = exp_peer(k)
        arrived(gath.at[q], sem_pick.at[q])

    loop(1, 16, wait_pick)

    total = jnp.zeros((128, 128), F32)
    for b in range(16):
        xb = gath[b].astype(F32).reshape(128, 128)
        total += xb * xb
    scale = lax.rsqrt(jnp.sum(total, axis=-1, keepdims=True) * (1.0 / D) + EPS)
    for b in range(16):
        xb = gath[b].astype(F32).reshape(128, 128)
        normed[:, b * 128 : (b + 1) * 128] = (xb * scale * again_ref[b : b + 1, :]).astype(BF)
    loads[0].wait()
    q_act, k_act, v_act = (dot(normed[...], wqkv[i]).astype(BF) for i in range(3))
    row_i = lax.broadcasted_iota(jnp.int32, (128, 128), 0)
    col_i = lax.broadcasted_iota(jnp.int32, (128, 128), 1)

    def sample_of(i):
        second = jnp.logical_or(jnp.logical_and(i >= 48, i < 96), i >= 112)
        return jnp.where(second, 1, 0)

    drop0 = dropped_ref[0]
    drop1 = dropped_ref[1]
    col_samp = sample_of(col_i)
    col_drop = jnp.where(col_samp == 1, drop1, drop0)
    col_kind = jnp.where(col_i >= 96, 2, 1)
    keep = jnp.logical_and(sample_of(row_i) == col_samp, col_drop != col_kind)
    scores = jnp.where(keep, dot_nt(q_act, k_act) * FACTOR, -1e30)
    weights = jnp.exp(scores - jnp.max(scores, axis=-1, keepdims=True))
    soft = weights / jnp.sum(weights, axis=-1, keepdims=True)
    probs32[...] = soft
    head_out = dot(soft.astype(BF), v_act).astype(BF)
    loads[1].wait()
    for b in range(4):
        cols = slice(b * 512, (b + 1) * 512)
        part[:, :, cols] = dot(head_out, wout[:, cols]).reshape(16, 8, 512).astype(BF)
    attr[e] = part[e]

    def send_attn(k):
        q, dev = exp_peer(k)
        send(part.at[q], attr.at[e], ssem.at[2], sem_attn.at[e], dev)

    loop(1, 16, send_attn)

    own_slot = ((c * 4 + x) * 2 + h) * 2 + zh

    def slot_of(core, q, z):
        return (core * 8 + q) * 2 + z

    def wait_cot(k):
        q, dev = exp_peer(k)
        arrived(cotg.at[q], sem_cot.at[q])

    loop(1, 16, wait_cot)
    own_iota = (lax.broadcasted_iota(jnp.int32, (8, 64), 0) + e * 8).astype(F32)
    cot_own = jnp.zeros((8, D), F32)
    for s in range(2):
        hot = jnp.where(own_iota == place[s : s + 1, :], 1.0, 0.0).astype(BF)
        rows = cotg[8 * s : 8 * s + 8].astype(F32).reshape(64, D).astype(BF)
        cot_own += dot(hot, rows)
    cotr[own_slot] = cot_own.astype(BF)

    def spread_first(buf, s_sem, r_sem):
        src = buf.at[own_slot]
        send(src, src, s_sem, r_sem.at[own_slot], zpart)

        def step(k):
            send(src, src, s_sem, r_sem.at[own_slot], xh_peer(k)[1])

        loop(1, 8, step)
        send(src, src, s_sem, r_sem.at[own_slot], sib)

    def spread_next(buf, s_sem, r_sem):
        other = slot_of(c, xh, 1 - zh)
        src = buf.at[other]
        arrived(src, r_sem.at[other])

        def step(k):
            send(src, src, s_sem, r_sem.at[other], xh_peer(k)[1])

        loop(1, 8, step)
        send(src, src, s_sem, r_sem.at[other], sib)

    def spread_last(buf, s_sem, r_sem):
        for z in (zh, 1 - zh):

            def step(k):
                slot = slot_of(c, (xh + 8 - k) % 8, z)
                arrived(buf.at[slot], r_sem.at[slot])
                send(buf.at[slot], buf.at[slot], s_sem, r_sem.at[slot], sib)

            loop(1, 8, step)

    def spread_done(buf, r_sem):
        def step(k):
            slot = (1 - c) * 16 + k
            arrived(buf.at[slot], r_sem.at[slot])

        loop(0, 16, step)

    spread_first(cotr, ssem.at[3], sem_cotr)
    for b in range(16):
        cols = slice(b * 128, (b + 1) * 128)
        norm_t[cols, :] = normed[:, cols].astype(F32).T.astype(BF)
    head_t = head_out.astype(F32).T.astype(BF)
    probs_t = soft.T.astype(BF)

    def wait_attn(k):
        q, dev = exp_peer(k)
        arrived(attr.at[q], sem_attn.at[q])

    loop(1, 16, wait_attn)
    own = jnp.concatenate([gath[b, e].astype(F32) for b in range(16)], axis=-1)
    attn_sum = attr[0].astype(F32)
    for b in range(1, 16):
        attn_sum += attr[b].astype(F32)
    residual = own + attn_sum
    res_scale = lax.rsqrt(jnp.mean(residual * residual, axis=-1, keepdims=True) + EPS)
    fgain = fgain_ref[...]
    tokg[own_slot] = (residual * res_scale * fgain).astype(BF)
    spread_first(tokg, ssem.at[4], sem_tok)
    spread_next(cotr, ssem.at[3], sem_cotr)
    spread_next(tokg, ssem.at[4], sem_tok)
    spread_last(cotr, ssem.at[3], sem_cotr)
    spread_last(tokg, ssem.at[4], sem_tok)
    spread_done(cotr, sem_cotr)

    def pack_rows(dst, buf):
        for b in range(8):
            rows = buf[4 * b : 4 * b + 4].astype(F32).reshape(32, D)
            dst[32 * b : 32 * b + 32, :] = rows.astype(BF)

    pack_rows(cmat, cotr)
    loads[2].wait()
    loads[3].wait()
    loads[4].wait()
    grad_hidden = dot_nt(cmat[...], wd[...])
    spread_done(tokg, sem_tok)
    pack_rows(tmat, tokg)
    gate = dot(tmat[...], wg[...])
    up = dot(tmat[...], wu[...])
    logistic = jax.nn.sigmoid(gate)
    active = gate * logistic
    hidden = (active * up).astype(BF)
    grad_gate = (grad_hidden * up * logistic * (1.0 + gate * (1.0 - logistic))).astype(BF)
    grad_up = (grad_hidden * active).astype(BF)
    for b in range(4):
        cols = slice(b * 512, (b + 1) * 512)
        osum[:, 0, :, cols] = dot(hidden, wd[:, cols]).reshape(32, 8, 512).astype(BF)
        back = dot_nt(grad_gate, wg[cols, :]) + dot_nt(grad_up, wu[cols, :])
        osum[:, 1, :, cols] = back.reshape(32, 8, 512).astype(BF)

    def d1_send(k):
        q = (xh + k) % 8
        send(
            osum.at[pl.ds(slot_of(1 - c, q, 0), 2)], r1.at[pl.ds(2 * q, 2)], ssem.at[5],
            sem_d1.at[q], sib,
        )

    loop(1, 9, d1_send)

    def d1_sum(q):
        arrived(r1.at[pl.ds(2 * q, 2)], sem_d1.at[q])
        for z in range(2):
            slot = 2 * q + z
            s1[slot] = (osum[c * 16 + slot].astype(F32) + r1[slot].astype(F32)).astype(BF)

    def d1_step(k):
        q, dev = xh_peer(k)
        d1_sum(q)
        send(s1.at[pl.ds(2 * q, 2)], r2.at[pl.ds(2 * xh, 2)], ssem.at[6], sem_d2.at[xh], dev)

    loop(1, 8, d1_step)
    d1_sum(xh)
    for z in range(2):
        r2[2 * xh + z] = s1[2 * xh + z]

    def wait_d2(k):
        q = (xh + k) % 8
        arrived(r2.at[pl.ds(2 * q, 2)], sem_d2.at[q])

    loop(1, 8, wait_d2)

    def d2_sum(z):
        acc = r2[z].astype(F32)
        for b in range(1, 8):
            acc += r2[2 * b + z].astype(F32)
        return acc

    s3[...] = d2_sum(1 - zh).astype(BF)
    send(s3, r3, ssem.at[7], sem_d3.at[0], zpart)
    sums = d2_sum(zh)
    arrived(r3, sem_d3.at[0])
    own_second = jnp.where(
        jnp.logical_or(jnp.logical_and(e >= 6, e < 12), e >= 14), drop1, drop0
    )
    own_kind = jnp.where(e >= 12, 2, 1)
    alive = jnp.where(own_second != own_kind, 1.0, 0.0)
    sums = (sums + r3[...].astype(F32)) * alive
    grad_in = sums[1] * fgain
    dot_mean = jnp.mean(residual * grad_in, axis=-1, keepdims=True)
    grad_norm = grad_in * res_scale - residual * (res_scale * res_scale * res_scale * dot_mean)
    grg[e] = (cot_own + grad_norm).astype(BF)

    def send_gr(k):
        q, dev = exp_peer(k)
        send(grg.at[e], grg.at[e], ssem.at[8], sem_gr.at[e], dev)

    loop(1, 16, send_gr)
    outg[e] = (residual + sums[0]).astype(BF)

    def send_out(k):
        q, dev = exp_peer(k)
        send(outg.at[e], outg.at[e], ssem.at[9], sem_out.at[e], dev)

    loop(1, 16, send_out)

    def wait_gr(k):
        q, dev = exp_peer(k)
        arrived(grg.at[q], sem_gr.at[q])

    loop(1, 16, wait_gr)

    for b in range(4):
        grmat[32 * b : 32 * b + 32, :] = (
            grg[4 * b : 4 * b + 4].astype(F32).reshape(32, D).astype(BF)
        )
    grad_att = dot_nt(grmat[...], wout[...]).astype(BF)
    soft_b = probs32[...]
    grad_probs = dot_nt(grad_att, v_act).astype(BF).astype(F32)
    grad_v = dot(probs_t, grad_att).astype(BF)
    row_sum = jnp.sum(grad_probs * soft_b, axis=-1, keepdims=True)
    grad_scores = soft_b * (grad_probs - row_sum)
    grad_q = (dot(grad_scores.astype(BF), k_act) * FACTOR).astype(BF)
    grad_k = (dot(grad_scores.T.astype(BF), q_act) * FACTOR).astype(BF)
    stacked = (grad_q, grad_k, grad_v)
    for j in range(12):
        f0 = (j % 4) * 512
        gbuf[j] = dot(norm_t[f0 : f0 + 512, :], stacked[j // 4]).astype(BF)
    for j in range(4):
        for b in range(4):
            c0 = (4 * j + b) * 128
            gbuf[12 + j, b * 128 : (b + 1) * 128, :] = dot(
                head_t, grmat[:, c0 : c0 + 128]
            ).astype(BF)

    def g1_send(k):
        q = (x + k) % 4
        send(
            gbuf.at[pl.ds((1 - c) * 8 + 2 * q, 2)], h1.at[pl.ds(2 * q, 2)], ssem.at[10],
            sem_g1.at[q], sib,
        )

    loop(1, 5, g1_send)

    def g1_sum(q):
        arrived(h1.at[pl.ds(2 * q, 2)], sem_g1.at[q])
        for z in range(2):
            i = 2 * q + z
            t1[i] = (gbuf[c * 8 + i].astype(F32) + h1[i].astype(F32)).astype(BF)

    def g1_step(k):
        q, dev = x_peer(k)
        g1_sum(q)
        send(t1.at[pl.ds(2 * q, 2)], h2.at[pl.ds(2 * x, 2)], ssem.at[11], sem_g2.at[x], dev)

    loop(1, 4, g1_step)
    g1_sum(x)
    for z in range(2):
        h2[2 * x + z] = t1[2 * x + z]

    def wait_g2(k):
        q = (x + k) % 4
        arrived(h2.at[pl.ds(2 * q, 2)], sem_g2.at[q])

    loop(1, 4, wait_g2)

    def g2_sum(z):
        acc = h2[z].astype(F32)
        for b in range(1, 4):
            acc += h2[2 * b + z].astype(F32)
        return acc

    t3[...] = g2_sum(1 - zh).astype(BF)
    send(t3, h3, ssem.at[12], sem_g3.at[0], zsame)
    seg_sum = g2_sum(zh)
    arrived(h3, sem_g3.at[0])
    seg = (c * 4 + x) * 2 + zh
    seg_z = (c * 4 + x) * 2 + 1 - zh
    gfin[seg] = (seg_sum + h3[...].astype(F32)).astype(BF)

    def fin(slot, dev):
        send(gfin.at[slot], gfin.at[slot], ssem.at[13], sem_fin.at[slot], dev)

    fin(seg, zsame)
    loop(1, 4, lambda k: fin(seg, x_peer(k)[1]))
    fin(seg, sib)

    def wait_out(k):
        q, dev = exp_peer(k)
        arrived(outg.at[q], sem_out.at[q])

    loop(1, 16, wait_out)
    row8 = lax.broadcasted_iota(jnp.int32, (8, 64), 0) + e * 8
    col8 = lax.broadcasted_iota(jnp.int32, (8, 64), 1)
    back_hot = jnp.zeros((8, 128), F32)
    for s in range(2):
        back_hot += dot_nt(jnp.where(row8 == col8 + 64 * s, 1.0, 0.0).astype(BF), place_hot[s])
    out_rows = outg[...].astype(F32).reshape(128, D).astype(BF)
    out_ref[...] = dot(back_hot.astype(BF), out_rows).astype(BF)

    arrived(gfin.at[seg_z], sem_fin.at[seg_z])
    loop(1, 4, lambda k: fin(seg_z, x_peer(k)[1]))
    fin(seg_z, sib)
    for z in (zh, 1 - zh):

        def fin_step(k):
            slot = (c * 4 + (x + 4 - k) % 4) * 2 + z
            arrived(gfin.at[slot], sem_fin.at[slot])
            fin(slot, sib)

        loop(1, 4, fin_step)

    def fin_wait(k):
        slot = (1 - c) * 8 + k
        arrived(gfin.at[slot], sem_fin.at[slot])

    loop(0, 8, fin_wait)

    sent(gath.at[pl.ds(0, 15)], ssem.at[0])
    sent(cotg.at[pl.ds(0, 15)], ssem.at[1])
    sent(attr.at[pl.ds(0, 15)], ssem.at[2])
    sent(cotr.at[pl.ds(0, 31)], ssem.at[3])
    sent(tokg.at[pl.ds(0, 31)], ssem.at[4])
    sent(r1, ssem.at[5])
    sent(r2.at[pl.ds(0, 14)], ssem.at[6])
    sent(r3, ssem.at[7])
    sent(grg.at[pl.ds(0, 15)], ssem.at[8])
    sent(outg.at[pl.ds(0, 15)], ssem.at[9])
    sent(h1, ssem.at[10])
    sent(h2.at[pl.ds(0, 6)], ssem.at[11])
    sent(h3, ssem.at[12])
    sent(gfin.at[pl.ds(0, 15)], ssem.at[13])


def layer(patches, visible, modality, dropped, again, w_qkv, w_out, fgain, wg, wu, wd, cot):
    vm = pl.BlockSpec(memory_space=pltpu.VMEM)
    anywhere = pl.BlockSpec(memory_space=pl.ANY)
    dma = pltpu.SemaphoreType.DMA
    scratch = [
        pltpu.VMEM((3, D, 128), BF),
        pltpu.VMEM((128, D), BF),
        pltpu.VMEM((D, 256), BF),
        pltpu.VMEM((D, 256), BF),
        pltpu.VMEM((256, D), BF),
        pltpu.VMEM((16, 16, 8, 128), BF),
        pltpu.VMEM((16, 8, D), BF),
        pltpu.VMEM((16, 8, D), BF),
        pltpu.VMEM((16, 8, D), BF),
        pltpu.VMEM((128, D), BF),
        pltpu.VMEM((D, 128), BF),
        pltpu.VMEM((128, 128), F32),
        pltpu.VMEM((32, 8, D), BF),
        pltpu.VMEM((32, 8, D), BF),
        pltpu.VMEM((256, D), BF),
        pltpu.VMEM((256, D), BF),
        pltpu.VMEM((32, 2, 8, D), BF),
        pltpu.VMEM((16, 2, 8, D), BF),
        pltpu.VMEM((16, 2, 8, D), BF),
        pltpu.VMEM((16, 2, 8, D), BF),
        pltpu.VMEM((2, 8, D), BF),
        pltpu.VMEM((2, 8, D), BF),
        pltpu.VMEM((16, 8, D), BF),
        pltpu.VMEM((16, 8, D), BF),
        pltpu.VMEM((128, D), BF),
        pltpu.VMEM((16, 512, 128), BF),
        pltpu.VMEM((8, 512, 128), BF),
        pltpu.VMEM((8, 512, 128), BF),
        pltpu.VMEM((8, 512, 128), BF),
        pltpu.VMEM((512, 128), BF),
        pltpu.VMEM((512, 128), BF),
        dma((5,)),
        dma((14,)),
        dma((16,)),
        dma((16,)),
        dma((16,)),
        dma((32,)),
        dma((32,)),
        dma((8,)),
        dma((8,)),
        dma((1,)),
        dma((16,)),
        dma((16,)),
        dma((4,)),
        dma((4,)),
        dma((1,)),
        dma((16,)),
    ]
    out, grads = pl.pallas_call(
        kernel,
        out_shape=(
            jax.ShapeDtypeStruct((8, D), BF),
            jax.ShapeDtypeStruct((16, 512, 128), BF),
        ),
        in_specs=[pl.BlockSpec(memory_space=pltpu.SMEM)] + [vm] * 6 + [anywhere] * 5,
        out_specs=(vm, vm),
        scratch_shapes=scratch,
        compiler_params=pltpu.CompilerParams(
            collective_id=0, has_side_effects=True, vmem_limit_bytes=56 * 1024 * 1024
        ),
        name="layer",
    )(
        dropped,
        patches,
        visible,
        modality,
        again.reshape(16, 128),
        fgain.reshape(1, D),
        cot,
        w_qkv.transpose(1, 0, 2),
        w_out,
        wg[0],
        wu[0],
        wd[0],
    )
    grad_qkv = grads[:12].reshape(3, D, 128).transpose(1, 0, 2).astype(F32)
    grad_out = grads[12:].reshape(16, 128, 128).transpose(1, 0, 2).reshape(128, D).astype(F32)
    return out, grad_qkv, grad_out


def solution(mesh):
    placed = (
        P("dp", None, "expert"),
        P("dp", None),
        P("dp", None),
        P("dp"),
        P(),
        P(None, None, "expert"),
        P("expert", None),
        P(),
        P("expert", None, "dp"),
        P("expert", None, "dp"),
        P("expert", "dp", None),
        P(("dp", "expert"), None),
    )
    return jax.shard_map(
        layer,
        mesh=mesh,
        in_specs=placed,
        out_specs=(P(("dp", "expert"), None), P(None, None, "expert"), P("expert", None)),
        check_vma=False,
    )
```

```python
import math

import jax
import jax.numpy as jnp
from jax import lax
from jax.experimental import pallas as pl
from jax.experimental.pallas import tpu as pltpu
from jax.sharding import PartitionSpec as P

BF = jnp.bfloat16
F32 = jnp.float32
MESH = pl.DeviceIdType.MESH
D = 2048
EPS = 1e-06
FACTOR = 1.0 / math.sqrt(128)


def dot(a, b):
    return jnp.dot(a, b, preferred_element_type=F32)


def dot_nt(a, b):
    return lax.dot_general(a, b, (((1,), (1,)), ((), ())), preferred_element_type=F32)


def kernel(
    dropped_ref,
    patches_ref,
    visible_ref,
    modality_ref,
    again_ref,
    fgain_ref,
    cot_ref,
    wqkv_hbm,
    wout_hbm,
    wg_hbm,
    wu_hbm,
    wd_hbm,
    out_ref,
    gq_fin,
    go_fin,
    wqkv,
    wout,
    wg,
    wu,
    wd,
    gath,
    cotg,
    part,
    party,
    zsum,
    partz,
    normed,
    norm_t,
    probs32,
    tokg,
    cotr,
    tmat,
    cmat,
    osum,
    r1,
    s1,
    r2,
    s3,
    r3,
    outg,
    grg,
    grmat,
    go_part,
    go_near,
    go_both,
    go_ring,
    go_out,
    go_in,
    gq_part,
    gq_near,
    gq_both,
    gq_ring,
    gq_out,
    gq_in,
    wsem,
    ssem,
    sem_pick,
    sem_cot,
    sem_ay,
    sem_az,
    sem_tok,
    sem_cotr,
    sem_d1,
    sem_d2,
    sem_d3,
    sem_gr,
    sem_out,
    sem_g1,
    sem_g2,
    sem_g3,
    sem_go,
    sem_q1,
    sem_q2,
    sem_q3,
    sem_gq,
):
    d = lax.axis_index("dp")
    e = lax.axis_index("expert")
    zh = d // 8
    x = (d // 2) % 4
    c = d % 2
    zl = e // 4
    y = e % 4
    h = y % 2
    xh = x * 2 + h
    sib = (zh * 8 + x * 2 + (1 - c), e)
    z_row = (1 - zh) * 8 + x * 2 + c
    zpart = (z_row, ((6 - zl) % 4) * 4 + y)
    zsame = (z_row, e)

    def exp_peer(k):
        q = (e + k) % 16
        return q, (d, q)

    def z_peer(k):
        q = (zl + k) % 4
        return q, (d, q * 4 + y)

    def y_peer(k):
        q = (y + k) % 4
        return q, (d, zl * 4 + q)

    def xh_peer(k):
        q = (xh + k) % 8
        return q, (zh * 8 + (q // 2) * 2 + c, zl * 4 + (y // 2) * 2 + q % 2)

    def x_peer(k):
        q = (x + k) % 4
        return q, (zh * 8 + q * 2 + c, e)

    def send(src, dst, s_sem, r_sem, dev):
        pltpu.make_async_remote_copy(
            src_ref=src, dst_ref=dst, send_sem=s_sem, recv_sem=r_sem,
            device_id=dev, device_id_type=MESH,
        ).start()

    def arrived(dst, r_sem):
        pltpu.make_async_remote_copy(
            src_ref=dst, dst_ref=dst, send_sem=ssem.at[0], recv_sem=r_sem,
            device_id=sib, device_id_type=MESH,
        ).wait_recv()

    def sent(src, s_sem):
        pltpu.make_async_remote_copy(
            src_ref=src, dst_ref=src, send_sem=s_sem, recv_sem=sem_d3.at[0],
            device_id=sib, device_id_type=MESH,
        ).wait_send()

    def loop(lo, hi, fn):
        def step(k, carry):
            fn(k)
            return carry

        lax.fori_loop(lo, hi, step, 0)

    def gather_z(buf, s_sem, r_sem):
        loop(1, 4, lambda k: send(buf.at[e], buf.at[e], s_sem, r_sem.at[e], z_peer(k)[1]))

    def gather_y(buf, s_sem, r_sem):
        loop(1, 4, lambda k: send(buf.at[e], buf.at[e], s_sem, r_sem.at[e], y_peer(k)[1]))

    def gather_next(buf, s_sem, r_sem):
        def step(j):
            slot = ((zl + 4 - j) % 4) * 4 + y
            arrived(buf.at[slot], r_sem.at[slot])
            loop(
                1, 4,
                lambda k: send(buf.at[slot], buf.at[slot], s_sem, r_sem.at[slot], y_peer(k)[1]),
            )

        loop(1, 4, step)

    def gather_done(buf, r_sem):
        def step(j):
            def inner(k):
                slot = ((zl + 4 - j) % 4) * 4 + (y + 4 - k) % 4
                arrived(buf.at[slot], r_sem.at[slot])

            loop(1, 4, inner)

        loop(0, 4, step)

    loads = [
        pltpu.make_async_copy(src, dst, wsem.at[i])
        for i, (src, dst) in enumerate(
            ((wqkv_hbm, wqkv), (wout_hbm, wout), (wg_hbm, wg), (wu_hbm, wu), (wd_hbm, wd))
        )
    ]
    for load in loads:
        load.start()

    barrier = pltpu.get_barrier_semaphore()

    def greet(dev):
        pl.semaphore_signal(barrier, inc=1, device_id=dev, device_id_type=MESH)

    loop(1, 16, lambda k: greet(exp_peer(k)[1]))
    loop(1, 8, lambda k: greet(xh_peer(k)[1]))
    greet(sib)
    greet(zpart)
    greet(zsame)

    mod = modality_ref[...].astype(F32)
    upto = (
        lax.broadcasted_iota(jnp.int32, (64, 64), 0) <= lax.broadcasted_iota(jnp.int32, (64, 64), 1)
    ).astype(F32)
    samp_col = lax.broadcasted_iota(jnp.int32, (2, 64), 0).astype(F32)
    rank_sar = dot(mod, upto) - 1.0
    rank_opt = dot(1.0 - mod, upto) - 1.0
    place = jnp.where(mod > 0.5, 96.0 + 16.0 * samp_col + rank_sar, 48.0 * samp_col + rank_opt)
    slot_iota = lax.broadcasted_iota(jnp.int32, (128, 64), 0).astype(F32)
    patch_iota = lax.broadcasted_iota(jnp.int32, (256, 64), 0)
    place_hot = [
        jnp.where(slot_iota == place[s : s + 1, :], 1.0, 0.0).astype(BF) for s in range(2)
    ]
    picked = jnp.zeros((128, 128), F32)
    for s in range(2):
        patch_hot = jnp.where(patch_iota == visible_ref[s : s + 1, :], 1.0, 0.0).astype(BF)
        picked += dot(dot_nt(place_hot[s], patch_hot).astype(BF), patches_ref[s])
    gath[e] = picked.reshape(16, 8, 128).astype(BF)
    cotg[e] = cot_ref[...]

    pl.semaphore_wait(barrier, 25)

    pick_sems = (ssem.at[0], sem_pick)
    cot_sems = (ssem.at[1], sem_cot)
    gather_z(gath, *pick_sems)
    gather_y(gath, *pick_sems)
    gather_next(gath, *pick_sems)
    gather_z(cotg, *cot_sems)
    gather_done(gath, sem_pick)
    gather_y(cotg, *cot_sems)
    gather_next(cotg, *cot_sems)

    total = jnp.zeros((128, 128), F32)
    for b in range(16):
        xb = gath[b].astype(F32).reshape(128, 128)
        total += xb * xb
    scale = lax.rsqrt(jnp.sum(total, axis=-1, keepdims=True) * (1.0 / D) + EPS)
    for b in range(16):
        xb = gath[b].astype(F32).reshape(128, 128)
        normed[:, b * 128 : (b + 1) * 128] = (xb * scale * again_ref[b : b + 1, :]).astype(BF)
    loads[0].wait()
    q_act, k_act, v_act = (dot(normed[...], wqkv[i]).astype(BF) for i in range(3))
    row_i = lax.broadcasted_iota(jnp.int32, (128, 128), 0)
    col_i = lax.broadcasted_iota(jnp.int32, (128, 128), 1)

    def sample_of(i):
        second = jnp.logical_or(jnp.logical_and(i >= 48, i < 96), i >= 112)
        return jnp.where(second, 1, 0)

    drop0 = dropped_ref[0]
    drop1 = dropped_ref[1]
    col_samp = sample_of(col_i)
    col_drop = jnp.where(col_samp == 1, drop1, drop0)
    col_kind = jnp.where(col_i >= 96, 2, 1)
    keep = jnp.logical_and(sample_of(row_i) == col_samp, col_drop != col_kind)
    scores = jnp.where(keep, dot_nt(q_act, k_act) * FACTOR, -1e30)
    weights = jnp.exp(scores - jnp.max(scores, axis=-1, keepdims=True))
    soft = weights / jnp.sum(weights, axis=-1, keepdims=True)
    probs32[...] = soft
    head_out = dot(soft.astype(BF), v_act).astype(BF)
    loads[1].wait()
    for b in range(4):
        cols = slice(b * 512, (b + 1) * 512)
        rows = dot(head_out, wout[:, cols]).reshape(16, 8, 512).astype(BF)
        for i in range(16):
            part[i % 4, i // 4, :, cols] = rows[i]
    party[y] = part[y]

    def send_attn(k):
        q, dev = y_peer(k)
        send(part.at[q], party.at[y], ssem.at[2], sem_ay.at[y], dev)

    loop(1, 4, send_attn)

    own_slot = (c * 2 + zh) * 8 + xh

    def slot_of(core, q, z):
        return (core * 2 + z) * 8 + q

    gather_done(cotg, sem_cot)
    own_iota = (lax.broadcasted_iota(jnp.int32, (8, 64), 0) + e * 8).astype(F32)
    cot_own = jnp.zeros((8, D), F32)
    for s in range(2):
        hot = jnp.where(own_iota == place[s : s + 1, :], 1.0, 0.0).astype(BF)
        rows = cotg[8 * s : 8 * s + 8].astype(F32).reshape(64, D).astype(BF)
        cot_own += dot(hot, rows)
    cotr[own_slot] = cot_own.astype(BF)

    def spread_first(buf, s_sem, r_sem):
        src = buf.at[own_slot]
        send(src, src, s_sem, r_sem.at[own_slot], zpart)

        def step(k):
            send(src, src, s_sem, r_sem.at[own_slot], xh_peer(k)[1])

        loop(1, 8, step)
        send(src, src, s_sem, r_sem.at[own_slot], sib)

    def spread_next(buf, s_sem, r_sem):
        other = slot_of(c, xh, 1 - zh)
        src = buf.at[other]
        arrived(src, r_sem.at[other])

        def step(k):
            send(src, src, s_sem, r_sem.at[other], xh_peer(k)[1])

        loop(1, 8, step)
        send(src, src, s_sem, r_sem.at[other], sib)

    def spread_last(buf, s_sem, r_sem):
        for z in (zh, 1 - zh):

            def step(k):
                slot = slot_of(c, (xh + 8 - k) % 8, z)
                arrived(buf.at[slot], r_sem.at[slot])
                send(buf.at[slot], buf.at[slot], s_sem, r_sem.at[slot], sib)

            loop(1, 8, step)

    def spread_done(buf, r_sem):
        def step(k):
            slot = (1 - c) * 16 + k
            arrived(buf.at[slot], r_sem.at[slot])

        loop(0, 16, step)

    spread_first(cotr, ssem.at[3], sem_cotr)
    for b in range(16):
        cols = slice(b * 128, (b + 1) * 128)
        norm_t[cols, :] = normed[:, cols].astype(F32).T.astype(BF)
    head_t = head_out.astype(F32).T.astype(BF)
    probs_t = soft.T.astype(BF)

    def wait_ay(k):
        q = (y + k) % 4
        arrived(party.at[q], sem_ay.at[q])

    loop(1, 4, wait_ay)

    def y_sum(z):
        acc = party[0, z].astype(F32)
        for b in range(1, 4):
            acc += party[b, z].astype(F32)
        return acc

    def send_az(k):
        q, dev = z_peer(k)
        zsum[q] = y_sum(q).astype(BF)
        send(zsum.at[q], partz.at[k - 1], ssem.at[14], sem_az.at[k - 1], dev)

    loop(1, 4, send_az)
    attn_sum = y_sum(zl)
    own = jnp.concatenate([gath[b, e].astype(F32) for b in range(16)], axis=-1)
    loop(0, 3, lambda k: arrived(partz.at[k], sem_az.at[k]))
    for b in range(3):
        attn_sum += partz[b].astype(F32)
    residual = own + attn_sum
    res_scale = lax.rsqrt(jnp.mean(residual * residual, axis=-1, keepdims=True) + EPS)
    fgain = fgain_ref[...]
    tokg[own_slot] = (residual * res_scale * fgain).astype(BF)
    spread_first(tokg, ssem.at[4], sem_tok)
    spread_next(cotr, ssem.at[3], sem_cotr)
    spread_next(tokg, ssem.at[4], sem_tok)
    spread_last(cotr, ssem.at[3], sem_cotr)
    spread_last(tokg, ssem.at[4], sem_tok)
    spread_done(cotr, sem_cotr)

    def pack_rows(dst, buf):
        for b in range(8):
            rows = buf[4 * b : 4 * b + 4].astype(F32).reshape(32, D)
            dst[32 * b : 32 * b + 32, :] = rows.astype(BF)

    pack_rows(cmat, cotr)
    loads[2].wait()
    loads[3].wait()
    loads[4].wait()
    grad_hidden = dot_nt(cmat[...], wd[...])
    spread_done(tokg, sem_tok)
    pack_rows(tmat, tokg)
    gate = dot(tmat[...], wg[...])
    up = dot(tmat[...], wu[...])
    logistic = jax.nn.sigmoid(gate)
    active = gate * logistic
    hidden = (active * up).astype(BF)
    grad_gate = (grad_hidden * up * logistic * (1.0 + gate * (1.0 - logistic))).astype(BF)
    grad_up = (grad_hidden * active).astype(BF)
    for b in range(4):
        cols = slice(b * 512, (b + 1) * 512)
        osum[:, 0, :, cols] = dot(hidden, wd[:, cols]).reshape(32, 8, 512).astype(BF)
        back = dot_nt(grad_gate, wg[cols, :]) + dot_nt(grad_up, wu[cols, :])
        osum[:, 1, :, cols] = back.reshape(32, 8, 512).astype(BF)

    def sum_start(buf, near, s_sem, r_sem, n, me):
        for z in (1 - zh, zh):

            def step(k):
                i = z * n + (me + k) % n
                send(buf.at[(1 - c) * 2 * n + i], near.at[i], s_sem, r_sem.at[i], sib)

            loop(1, n + 1, step)

    def sum_next(buf, near, both, ring, s_sem, near_sem, ring_sem, n, me, peer):
        for z in (1 - zh, zh):

            def add(q):
                i = z * n + q
                arrived(near.at[i], near_sem.at[i])
                return (buf[c * 2 * n + i].astype(F32) + near[i].astype(F32)).astype(BF)

            def step(k):
                q, dev = peer(k)
                i = z * n + q
                both[i] = add(q)
                send(both.at[i], ring.at[z * n + me], s_sem, ring_sem.at[z * n + me], dev)

            loop(1, n, step)
            ring[z * n + me] = add(me)

    def ring_sum(ring, ring_sem, n, me, z):
        def step(k):
            i = z * n + (me + k) % n
            arrived(ring.at[i], ring_sem.at[i])

        loop(1, n, step)
        acc = ring[z * n].astype(F32)
        for b in range(1, n):
            acc += ring[z * n + b].astype(F32)
        return acc

    def sum_far(ring, far_out, far_in, s_sem, ring_sem, far_sem, n, me, dev):
        far_out[...] = ring_sum(ring, ring_sem, n, me, 1 - zh).astype(BF)
        send(far_out, far_in, s_sem, far_sem.at[0], dev)

    sum_start(osum, r1, ssem.at[5], sem_d1, 8, xh)
    sum_next(osum, r1, s1, r2, ssem.at[6], sem_d1, sem_d2, 8, xh, xh_peer)
    sum_far(r2, s3, r3, ssem.at[7], sem_d2, sem_d3, 8, xh, zpart)
    sums = ring_sum(r2, sem_d2, 8, xh, zh)
    arrived(r3, sem_d3.at[0])
    own_second = jnp.where(
        jnp.logical_or(jnp.logical_and(e >= 6, e < 12), e >= 14), drop1, drop0
    )
    own_kind = jnp.where(e >= 12, 2, 1)
    alive = jnp.where(own_second != own_kind, 1.0, 0.0)
    sums = (sums + r3[...].astype(F32)) * alive
    grad_in = sums[1] * fgain
    dot_mean = jnp.mean(residual * grad_in, axis=-1, keepdims=True)
    grad_norm = grad_in * res_scale - residual * (res_scale * res_scale * res_scale * dot_mean)
    grg[e] = (cot_own + grad_norm).astype(BF)

    gr_sems = (ssem.at[8], sem_gr)
    out_sems = (ssem.at[9], sem_out)
    gather_z(grg, *gr_sems)
    gather_y(grg, *gr_sems)
    outg[e] = (residual + sums[0]).astype(BF)
    gather_next(grg, *gr_sems)
    gather_z(outg, *out_sems)
    gather_done(grg, sem_gr)

    for b in range(4):
        grmat[32 * b : 32 * b + 32, :] = (
            grg[4 * b : 4 * b + 4].astype(F32).reshape(32, D).astype(BF)
        )
    for b in range(8):
        pair = dot(head_t, grmat[:, b * 256 : (b + 1) * 256]).astype(BF)
        go_part[2 * b] = pair[:, :128]
        go_part[2 * b + 1] = pair[:, 128:]
    sum_start(go_part, go_near, ssem.at[10], sem_g1, 4, x)
    gather_y(outg, *out_sems)
    gather_next(outg, *out_sems)
    grad_att = dot_nt(grmat[...], wout[...]).astype(BF)
    soft_b = probs32[...]
    grad_probs = dot_nt(grad_att, v_act).astype(BF).astype(F32)
    grad_v = dot(probs_t, grad_att).astype(BF)
    sum_next(
        go_part, go_near, go_both, go_ring, ssem.at[11], sem_g1, sem_g2, 4, x, x_peer
    )
    row_sum = jnp.sum(grad_probs * soft_b, axis=-1, keepdims=True)
    grad_scores = soft_b * (grad_probs - row_sum)
    grad_q = (dot(grad_scores.astype(BF), k_act) * FACTOR).astype(BF)
    grad_k = (dot(grad_scores.T.astype(BF), q_act) * FACTOR).astype(BF)
    stacked = (grad_q, grad_k, grad_v)
    for j in range(16):
        row = 384 * j
        while row < 384 * (j + 1):
            upto_row = min(384 * (j + 1), (row // D + 1) * D)
            f0 = row % D
            gq_part[j, row - 384 * j : upto_row - 384 * j, :] = dot(
                norm_t[f0 : f0 + upto_row - row, :], stacked[row // D]
            ).astype(BF)
            row = upto_row
    sum_start(gq_part, gq_near, ssem.at[15], sem_q1, 4, x)
    sum_far(go_ring, go_out, go_in, ssem.at[12], sem_g2, sem_g3, 4, x, zsame)
    sum_next(
        gq_part, gq_near, gq_both, gq_ring, ssem.at[16], sem_q1, sem_q2, 4, x, x_peer
    )
    seg = (c * 2 + zh) * 4 + x
    seg_z = (c * 2 + 1 - zh) * 4 + x

    def sum_own(ring, far_in, fin, ring_sem, far_sem):
        acc = ring_sum(ring, ring_sem, 4, x, zh)
        arrived(far_in, far_sem.at[0])
        fin[seg] = (acc + far_in[...].astype(F32)).astype(BF)

    def fin_send(fin, slot, s_sem, r_sem, dev):
        send(fin.at[slot], fin.at[slot], s_sem, r_sem.at[slot], dev)

    def fin_first(fin, s_sem, r_sem):
        fin_send(fin, seg, s_sem, r_sem, zsame)
        loop(1, 4, lambda k: fin_send(fin, seg, s_sem, r_sem, x_peer(k)[1]))
        fin_send(fin, seg, s_sem, r_sem, sib)

    def fin_next(fin, s_sem, r_sem):
        arrived(fin.at[seg_z], r_sem.at[seg_z])
        loop(1, 4, lambda k: fin_send(fin, seg_z, s_sem, r_sem, x_peer(k)[1]))
        fin_send(fin, seg_z, s_sem, r_sem, sib)

    def fin_last(fin, s_sem, r_sem, z):
        def step(k):
            slot = (c * 2 + z) * 4 + (x + 4 - k) % 4
            arrived(fin.at[slot], r_sem.at[slot])
            fin_send(fin, slot, s_sem, r_sem, sib)

        loop(1, 4, step)

    def fin_done(fin, r_sem):
        def step(k):
            slot = (1 - c) * 8 + k
            arrived(fin.at[slot], r_sem.at[slot])

        loop(0, 8, step)

    go_sems = (ssem.at[13], sem_go)
    gq_sems = (ssem.at[18], sem_gq)
    sum_own(go_ring, go_in, go_fin, sem_g2, sem_g3)
    fin_first(go_fin, *go_sems)
    sum_far(gq_ring, gq_out, gq_in, ssem.at[17], sem_q2, sem_q3, 4, x, zsame)
    sum_own(gq_ring, gq_in, gq_fin, sem_q2, sem_q3)
    fin_first(gq_fin, *gq_sems)

    gather_done(outg, sem_out)
    row8 = lax.broadcasted_iota(jnp.int32, (8, 64), 0) + e * 8
    col8 = lax.broadcasted_iota(jnp.int32, (8, 64), 1)
    back_hot = jnp.zeros((8, 128), F32)
    for s in range(2):
        back_hot += dot_nt(jnp.where(row8 == col8 + 64 * s, 1.0, 0.0).astype(BF), place_hot[s])
    out_rows = outg[...].astype(F32).reshape(128, D).astype(BF)
    out_ref[...] = dot(back_hot.astype(BF), out_rows).astype(BF)

    fin_next(go_fin, *go_sems)
    fin_last(go_fin, *go_sems, zh)
    fin_last(gq_fin, *gq_sems, zh)
    fin_next(gq_fin, *gq_sems)
    fin_last(go_fin, *go_sems, 1 - zh)
    fin_last(gq_fin, *gq_sems, 1 - zh)
    fin_done(go_fin, sem_go)
    fin_done(gq_fin, sem_gq)

    sent(gath.at[pl.ds(0, 15)], ssem.at[0])
    sent(cotg.at[pl.ds(0, 15)], ssem.at[1])
    sent(party.at[pl.ds(0, 3)], ssem.at[2])
    sent(partz, ssem.at[14])
    sent(cotr.at[pl.ds(0, 31)], ssem.at[3])
    sent(tokg.at[pl.ds(0, 31)], ssem.at[4])
    sent(r1, ssem.at[5])
    sent(r2.at[pl.ds(0, 14)], ssem.at[6])
    sent(r3, ssem.at[7])
    sent(grg.at[pl.ds(0, 15)], ssem.at[8])
    sent(outg.at[pl.ds(0, 15)], ssem.at[9])
    sent(go_near, ssem.at[10])
    sent(go_ring.at[pl.ds(0, 6)], ssem.at[11])
    sent(go_in, ssem.at[12])
    sent(go_fin.at[pl.ds(0, 15)], ssem.at[13])
    sent(gq_near, ssem.at[15])
    sent(gq_ring.at[pl.ds(0, 6)], ssem.at[16])
    sent(gq_in, ssem.at[17])
    sent(gq_fin.at[pl.ds(0, 15)], ssem.at[18])


def layer(patches, visible, modality, dropped, again, w_qkv, w_out, fgain, wg, wu, wd, cot):
    vm = pl.BlockSpec(memory_space=pltpu.VMEM)
    anywhere = pl.BlockSpec(memory_space=pl.ANY)
    dma = pltpu.SemaphoreType.DMA
    scratch = [
        pltpu.VMEM((3, D, 128), BF),
        pltpu.VMEM((128, D), BF),
        pltpu.VMEM((D, 256), BF),
        pltpu.VMEM((D, 256), BF),
        pltpu.VMEM((256, D), BF),
        pltpu.VMEM((16, 16, 8, 128), BF),
        pltpu.VMEM((16, 8, D), BF),
        pltpu.VMEM((4, 4, 8, D), BF),
        pltpu.VMEM((4, 4, 8, D), BF),
        pltpu.VMEM((4, 8, D), BF),
        pltpu.VMEM((3, 8, D), BF),
        pltpu.VMEM((128, D), BF),
        pltpu.VMEM((D, 128), BF),
        pltpu.VMEM((128, 128), F32),
        pltpu.VMEM((32, 8, D), BF),
        pltpu.VMEM((32, 8, D), BF),
        pltpu.VMEM((256, D), BF),
        pltpu.VMEM((256, D), BF),
        pltpu.VMEM((32, 2, 8, D), BF),
        pltpu.VMEM((16, 2, 8, D), BF),
        pltpu.VMEM((16, 2, 8, D), BF),
        pltpu.VMEM((16, 2, 8, D), BF),
        pltpu.VMEM((2, 8, D), BF),
        pltpu.VMEM((2, 8, D), BF),
        pltpu.VMEM((16, 8, D), BF),
        pltpu.VMEM((16, 8, D), BF),
        pltpu.VMEM((128, D), BF),
        pltpu.VMEM((16, 128, 128), BF),
        pltpu.VMEM((8, 128, 128), BF),
        pltpu.VMEM((8, 128, 128), BF),
        pltpu.VMEM((8, 128, 128), BF),
        pltpu.VMEM((128, 128), BF),
        pltpu.VMEM((128, 128), BF),
        pltpu.VMEM((16, 384, 128), BF),
        pltpu.VMEM((8, 384, 128), BF),
        pltpu.VMEM((8, 384, 128), BF),
        pltpu.VMEM((8, 384, 128), BF),
        pltpu.VMEM((384, 128), BF),
        pltpu.VMEM((384, 128), BF),
        dma((5,)),
        dma((19,)),
        dma((16,)),
        dma((16,)),
        dma((4,)),
        dma((3,)),
        dma((32,)),
        dma((32,)),
        dma((16,)),
        dma((16,)),
        dma((1,)),
        dma((16,)),
        dma((16,)),
        dma((8,)),
        dma((8,)),
        dma((1,)),
        dma((16,)),
        dma((8,)),
        dma((8,)),
        dma((1,)),
        dma((16,)),
    ]
    out, gq, go = pl.pallas_call(
        kernel,
        out_shape=(
            jax.ShapeDtypeStruct((8, D), BF),
            jax.ShapeDtypeStruct((16, 384, 128), BF),
            jax.ShapeDtypeStruct((16, 128, 128), BF),
        ),
        in_specs=[pl.BlockSpec(memory_space=pltpu.SMEM)] + [vm] * 6 + [anywhere] * 5,
        out_specs=(vm, vm, vm),
        scratch_shapes=scratch,
        compiler_params=pltpu.CompilerParams(
            collective_id=0, has_side_effects=True, vmem_limit_bytes=56 * 1024 * 1024
        ),
        name="layer",
    )(
        dropped,
        patches,
        visible,
        modality,
        again.reshape(16, 128),
        fgain.reshape(1, D),
        cot,
        w_qkv.transpose(1, 0, 2),
        w_out,
        wg[0],
        wu[0],
        wd[0],
    )
    grad_qkv = gq.reshape(3, D, 128).transpose(1, 0, 2).astype(F32)
    grad_out = go.transpose(1, 0, 2).reshape(128, D).astype(F32)
    return out, grad_qkv, grad_out


def solution(mesh):
    placed = (
        P("dp", None, "expert"),
        P("dp", None),
        P("dp", None),
        P("dp"),
        P(),
        P(None, None, "expert"),
        P("expert", None),
        P(),
        P("expert", None, "dp"),
        P("expert", None, "dp"),
        P("expert", "dp", None),
        P(("dp", "expert"), None),
    )
    return jax.shard_map(
        layer,
        mesh=mesh,
        in_specs=placed,
        out_specs=(P(("dp", "expert"), None), P(None, None, "expert"), P("expert", None)),
        check_vma=False,
    )
```

```python
import math

import jax
import jax.numpy as jnp
from jax import lax
from jax.experimental import pallas as pl
from jax.experimental.pallas import tpu as pltpu
from jax.sharding import PartitionSpec as P

BF = jnp.bfloat16
F32 = jnp.float32
MESH = pl.DeviceIdType.MESH
D = 2048
EPS = 1e-06
FACTOR = 1.0 / math.sqrt(128)


def dot(a, b):
    return jnp.dot(a, b, preferred_element_type=F32)


def dot_nt(a, b):
    return lax.dot_general(a, b, (((1,), (1,)), ((), ())), preferred_element_type=F32)


def kernel(
    dropped_ref,
    patches_ref,
    visible_ref,
    modality_ref,
    again_ref,
    fgain_ref,
    cot_ref,
    wqkv_hbm,
    wout_hbm,
    wg_hbm,
    wu_hbm,
    wd_hbm,
    out_ref,
    gq_fin,
    go_fin,
    wqkv,
    wout,
    wg,
    wu,
    wd,
    gath,
    cotg,
    part,
    party,
    zsum,
    partz,
    normed,
    norm_t,
    probs32,
    tokg,
    cotr,
    tmat,
    cmat,
    osum,
    r1,
    s1,
    r2,
    s3,
    r3,
    outg,
    grg,
    grmat,
    go_part,
    go_near,
    go_both,
    go_ring,
    go_out,
    go_in,
    gq_part,
    gq_near,
    gq_both,
    gq_ring,
    gq_out,
    gq_in,
    wsem,
    ssem,
    sem_pick,
    sem_cot,
    sem_ay,
    sem_az,
    sem_tok,
    sem_cotr,
    sem_d1,
    sem_d2,
    sem_d3,
    sem_gr,
    sem_out,
    sem_g1,
    sem_g2,
    sem_g3,
    sem_go,
    sem_q1,
    sem_q2,
    sem_q3,
    sem_gq,
):
    d = lax.axis_index("dp")
    e = lax.axis_index("expert")
    zh = d // 8
    x = (d // 2) % 4
    c = d % 2
    zl = e // 4
    y = e % 4
    h = y % 2
    xh = x * 2 + h
    sib = (zh * 8 + x * 2 + (1 - c), e)
    z_row = (1 - zh) * 8 + x * 2 + c
    zpart = (z_row, ((6 - zl) % 4) * 4 + y)
    zsame = (z_row, e)

    def z_peer(k):
        q = (zl + k) % 4
        return q, (d, q * 4 + y)

    def y_peer(k):
        q = (y + k) % 4
        return q, (d, zl * 4 + q)

    def xh_peer(k):
        q = (xh + k) % 8
        return q, (zh * 8 + (q // 2) * 2 + c, zl * 4 + (y // 2) * 2 + q % 2)

    def x_peer(k):
        q = (x + k) % 4
        return q, (zh * 8 + q * 2 + c, e)

    def send(src, dst, s_sem, r_sem, dev):
        pltpu.make_async_remote_copy(
            src_ref=src, dst_ref=dst, send_sem=s_sem, recv_sem=r_sem,
            device_id=dev, device_id_type=MESH,
        ).start()

    def arrived(dst, r_sem):
        pltpu.make_async_remote_copy(
            src_ref=dst, dst_ref=dst, send_sem=ssem.at[0], recv_sem=r_sem,
            device_id=sib, device_id_type=MESH,
        ).wait_recv()

    def sent(src, s_sem):
        pltpu.make_async_remote_copy(
            src_ref=src, dst_ref=src, send_sem=s_sem, recv_sem=sem_d3.at[0],
            device_id=sib, device_id_type=MESH,
        ).wait_send()

    def loop(lo, hi, fn):
        def step(k, carry):
            fn(k)
            return carry

        lax.fori_loop(lo, hi, step, 0)

    def gather_z(buf, s_sem, r_sem):
        loop(1, 4, lambda k: send(buf.at[e], buf.at[e], s_sem, r_sem.at[e], z_peer(k)[1]))

    def gather_y(buf, s_sem, r_sem):
        loop(1, 4, lambda k: send(buf.at[e], buf.at[e], s_sem, r_sem.at[e], y_peer(k)[1]))

    def gather_next(buf, s_sem, r_sem):
        def step(j):
            slot = ((zl + 4 - j) % 4) * 4 + y
            arrived(buf.at[slot], r_sem.at[slot])
            loop(
                1, 4,
                lambda k: send(buf.at[slot], buf.at[slot], s_sem, r_sem.at[slot], y_peer(k)[1]),
            )

        loop(1, 4, step)

    def gather_done(buf, r_sem):
        def step(j):
            def inner(k):
                slot = ((zl + 4 - j) % 4) * 4 + (y + 4 - k) % 4
                arrived(buf.at[slot], r_sem.at[slot])

            loop(1, 4, inner)

        loop(0, 4, step)

    loads = [
        pltpu.make_async_copy(src, dst, wsem.at[i])
        for i, (src, dst) in enumerate(
            ((wqkv_hbm, wqkv), (wout_hbm, wout), (wg_hbm, wg), (wu_hbm, wu), (wd_hbm, wd))
        )
    ]
    for load in loads:
        load.start()

    barrier = pltpu.get_barrier_semaphore()

    def greet(dev):
        pl.semaphore_signal(barrier, inc=1, device_id=dev, device_id_type=MESH)

    loop(1, 4, lambda k: greet(z_peer(k)[1]))
    loop(1, 4, lambda k: greet(y_peer(k)[1]))
    loop(1, 8, lambda k: greet(xh_peer(k)[1]))
    greet(sib)
    greet(zpart)
    greet(zsame)

    mod = modality_ref[...].astype(F32)
    upto = (
        lax.broadcasted_iota(jnp.int32, (64, 64), 0) <= lax.broadcasted_iota(jnp.int32, (64, 64), 1)
    ).astype(F32)
    samp_col = lax.broadcasted_iota(jnp.int32, (2, 64), 0).astype(F32)
    rank_sar = dot(mod, upto) - 1.0
    rank_opt = dot(1.0 - mod, upto) - 1.0
    place = jnp.where(mod > 0.5, 96.0 + 16.0 * samp_col + rank_sar, 48.0 * samp_col + rank_opt)
    slot_iota = lax.broadcasted_iota(jnp.int32, (128, 64), 0).astype(F32)
    patch_iota = lax.broadcasted_iota(jnp.int32, (256, 64), 0)
    place_hot = [
        jnp.where(slot_iota == place[s : s + 1, :], 1.0, 0.0).astype(BF) for s in range(2)
    ]
    picked = jnp.zeros((128, 128), F32)
    for s in range(2):
        patch_hot = jnp.where(patch_iota == visible_ref[s : s + 1, :], 1.0, 0.0).astype(BF)
        picked += dot(dot_nt(place_hot[s], patch_hot).astype(BF), patches_ref[s])
    gath[e] = picked.reshape(16, 8, 128).astype(BF)
    cotg[e] = cot_ref[...]

    pl.semaphore_wait(barrier, 16)

    pick_sems = (ssem.at[0], sem_pick)
    cot_sems = (ssem.at[1], sem_cot)
    gather_z(gath, *pick_sems)
    gather_y(gath, *pick_sems)
    gather_next(gath, *pick_sems)
    gather_z(cotg, *cot_sems)
    gather_y(cotg, *cot_sems)
    gather_next(cotg, *cot_sems)
    gather_done(gath, sem_pick)

    total = jnp.zeros((128, 128), F32)
    for b in range(16):
        xb = gath[b].astype(F32).reshape(128, 128)
        total += xb * xb
    scale = lax.rsqrt(jnp.sum(total, axis=-1, keepdims=True) * (1.0 / D) + EPS)
    for b in range(16):
        xb = gath[b].astype(F32).reshape(128, 128)
        normed[:, b * 128 : (b + 1) * 128] = (xb * scale * again_ref[b : b + 1, :]).astype(BF)
    loads[0].wait()
    q_act, k_act, v_act = (dot(normed[...], wqkv[i]).astype(BF) for i in range(3))
    row_i = lax.broadcasted_iota(jnp.int32, (128, 128), 0)
    col_i = lax.broadcasted_iota(jnp.int32, (128, 128), 1)

    def sample_of(i):
        second = jnp.logical_or(jnp.logical_and(i >= 48, i < 96), i >= 112)
        return jnp.where(second, 1, 0)

    drop0 = dropped_ref[0]
    drop1 = dropped_ref[1]
    col_samp = sample_of(col_i)
    col_drop = jnp.where(col_samp == 1, drop1, drop0)
    col_kind = jnp.where(col_i >= 96, 2, 1)
    keep = jnp.logical_and(sample_of(row_i) == col_samp, col_drop != col_kind)
    scores = jnp.where(keep, dot_nt(q_act, k_act) * FACTOR, -1e30)
    weights = jnp.exp(scores - jnp.max(scores, axis=-1, keepdims=True))
    soft = weights / jnp.sum(weights, axis=-1, keepdims=True)
    probs32[...] = soft
    head_out = dot(soft.astype(BF), v_act).astype(BF)
    loads[1].wait()
    for b in range(4):
        cols = slice(b * 512, (b + 1) * 512)
        rows = dot(head_out, wout[:, cols]).reshape(16, 8, 512).astype(BF)
        for i in range(16):
            part[i % 4, i // 4, :, cols] = rows[i]
    party[y] = part[y]

    def send_attn(k):
        q, dev = y_peer(k)
        send(part.at[q], party.at[y], ssem.at[2], sem_ay.at[y], dev)

    loop(1, 4, send_attn)

    own_slot = (c * 2 + zh) * 8 + xh

    def slot_of(core, q, z):
        return (core * 2 + z) * 8 + q

    gather_done(cotg, sem_cot)
    own_iota = (lax.broadcasted_iota(jnp.int32, (8, 64), 0) + e * 8).astype(F32)
    cot_own = jnp.zeros((8, D), F32)
    for s in range(2):
        hot = jnp.where(own_iota == place[s : s + 1, :], 1.0, 0.0).astype(BF)
        rows = cotg[8 * s : 8 * s + 8].astype(F32).reshape(64, D).astype(BF)
        cot_own += dot(hot, rows)
    cotr[own_slot] = cot_own.astype(BF)

    def spread_first(buf, s_sem, r_sem):
        src = buf.at[own_slot]
        send(src, src, s_sem, r_sem.at[own_slot], zpart)

        def step(k):
            send(src, src, s_sem, r_sem.at[own_slot], xh_peer(k)[1])

        loop(1, 8, step)
        send(src, src, s_sem, r_sem.at[own_slot], sib)

    def spread_next(buf, s_sem, r_sem):
        other = slot_of(c, xh, 1 - zh)
        src = buf.at[other]
        arrived(src, r_sem.at[other])

        def step(k):
            send(src, src, s_sem, r_sem.at[other], xh_peer(k)[1])

        loop(1, 8, step)
        send(src, src, s_sem, r_sem.at[other], sib)

    def spread_last(buf, s_sem, r_sem):
        for z in (zh, 1 - zh):

            def step(k):
                slot = slot_of(c, (xh + 8 - k) % 8, z)
                arrived(buf.at[slot], r_sem.at[slot])
                send(buf.at[slot], buf.at[slot], s_sem, r_sem.at[slot], sib)

            loop(1, 8, step)

    def spread_done(buf, r_sem):
        def step(k):
            slot = (1 - c) * 16 + k
            arrived(buf.at[slot], r_sem.at[slot])

        loop(0, 16, step)

    h_peer = (d, zl * 4 + y + 1 - 2 * h)

    def share(buf, slot, s_sem, r_sem, devs):
        src = buf.at[slot]
        for dev in devs:
            send(src, src, s_sem, r_sem.at[slot], dev)
        loop(1, 4, lambda k: send(src, src, s_sem, r_sem.at[slot], x_peer(k)[1]))

    share(cotr, own_slot, ssem.at[3], sem_cotr, (zpart, h_peer, sib))
    for b in range(16):
        cols = slice(b * 128, (b + 1) * 128)
        norm_t[cols, :] = normed[:, cols].astype(F32).T.astype(BF)
    head_t = head_out.astype(F32).T.astype(BF)
    probs_t = soft.T.astype(BF)

    def cot_pass(slot, devs):
        arrived(cotr.at[slot], sem_cotr.at[slot])
        share(cotr, slot, ssem.at[3], sem_cotr, devs)

    def cot_rest():
        for z in (zh, 1 - zh):
            for other in (0, 1):

                def step(k):
                    row = (x + 4 - k) % 4 * 2
                    slot = slot_of(c, row + (h if other == 0 else 1 - h), z)
                    arrived(cotr.at[slot], sem_cotr.at[slot])
                    send(cotr.at[slot], cotr.at[slot], ssem.at[3], sem_cotr.at[slot], sib)

                loop(1, 4, step)

    def wait_ay(k):
        q = (y + k) % 4
        arrived(party.at[q], sem_ay.at[q])

    loop(1, 4, wait_ay)

    def y_sum(z):
        acc = party[0, z].astype(F32)
        for b in range(1, 4):
            acc += party[b, z].astype(F32)
        return acc

    def send_az(k):
        q, dev = z_peer(k)
        zsum[q] = y_sum(q).astype(BF)
        send(zsum.at[q], partz.at[k - 1], ssem.at[14], sem_az.at[k - 1], dev)

    loop(1, 4, send_az)
    cot_pass(slot_of(c, xh, 1 - zh), (h_peer, sib))
    cot_pass(slot_of(c, x * 2 + 1 - h, zh), (sib,))
    cot_pass(slot_of(c, x * 2 + 1 - h, 1 - zh), (sib,))
    attn_sum = y_sum(zl)
    own = jnp.concatenate([gath[b, e].astype(F32) for b in range(16)], axis=-1)
    loop(0, 3, lambda k: arrived(partz.at[k], sem_az.at[k]))
    for b in range(3):
        attn_sum += partz[b].astype(F32)
    residual = own + attn_sum
    res_scale = lax.rsqrt(jnp.mean(residual * residual, axis=-1, keepdims=True) + EPS)
    fgain = fgain_ref[...]
    tokg[own_slot] = (residual * res_scale * fgain).astype(BF)
    spread_first(tokg, ssem.at[4], sem_tok)
    spread_next(tokg, ssem.at[4], sem_tok)
    cot_rest()
    spread_last(tokg, ssem.at[4], sem_tok)
    spread_done(cotr, sem_cotr)

    def pack_rows(dst, buf):
        for b in range(8):
            rows = buf[4 * b : 4 * b + 4].astype(F32).reshape(32, D)
            dst[32 * b : 32 * b + 32, :] = rows.astype(BF)

    pack_rows(cmat, cotr)
    loads[2].wait()
    loads[3].wait()
    loads[4].wait()
    grad_hidden = dot_nt(cmat[...], wd[...])
    spread_done(tokg, sem_tok)
    pack_rows(tmat, tokg)
    gate = dot(tmat[...], wg[...])
    up = dot(tmat[...], wu[...])
    logistic = jax.nn.sigmoid(gate)
    active = gate * logistic
    hidden = (active * up).astype(BF)
    grad_gate = (grad_hidden * up * logistic * (1.0 + gate * (1.0 - logistic))).astype(BF)
    grad_up = (grad_hidden * active).astype(BF)
    for b in range(4):
        cols = slice(b * 512, (b + 1) * 512)
        osum[:, 0, :, cols] = dot(hidden, wd[:, cols]).reshape(32, 8, 512).astype(BF)
        back = dot_nt(grad_gate, wg[cols, :]) + dot_nt(grad_up, wu[cols, :])
        osum[:, 1, :, cols] = back.reshape(32, 8, 512).astype(BF)

    def sum_start(buf, near, s_sem, r_sem, n, me, halves):
        for z in halves:

            def step(k):
                i = z * n + (me + k) % n
                send(buf.at[(1 - c) * 2 * n + i], near.at[i], s_sem, r_sem.at[i], sib)

            loop(1, n + 1, step)

    def sum_next(buf, near, both, ring, s_sem, near_sem, ring_sem, n, me, peer, halves):
        for z in halves:

            def add(q):
                i = z * n + q
                arrived(near.at[i], near_sem.at[i])
                return (buf[c * 2 * n + i].astype(F32) + near[i].astype(F32)).astype(BF)

            def step(k):
                q, dev = peer(k)
                i = z * n + q
                both[i] = add(q)
                send(both.at[i], ring.at[z * n + me], s_sem, ring_sem.at[z * n + me], dev)

            loop(1, n, step)
            ring[z * n + me] = add(me)

    def ring_sum(ring, ring_sem, n, me, z):
        def step(k):
            i = z * n + (me + k) % n
            arrived(ring.at[i], ring_sem.at[i])

        loop(1, n, step)
        acc = ring[z * n].astype(F32)
        for b in range(1, n):
            acc += ring[z * n + b].astype(F32)
        return acc

    sum_start(osum, r1, ssem.at[5], sem_d1, 8, xh, (1 - zh, zh))
    sum_next(osum, r1, s1, r2, ssem.at[6], sem_d1, sem_d2, 8, xh, xh_peer, (1 - zh, zh))
    s3[...] = ring_sum(r2, sem_d2, 8, xh, 1 - zh).astype(BF)
    send(s3, r3, ssem.at[7], sem_d3.at[0], zpart)
    sums = ring_sum(r2, sem_d2, 8, xh, zh)
    arrived(r3, sem_d3.at[0])
    own_second = jnp.where(
        jnp.logical_or(jnp.logical_and(e >= 6, e < 12), e >= 14), drop1, drop0
    )
    own_kind = jnp.where(e >= 12, 2, 1)
    alive = jnp.where(own_second != own_kind, 1.0, 0.0)
    sums = (sums + r3[...].astype(F32)) * alive
    grad_in = sums[1] * fgain
    dot_mean = jnp.mean(residual * grad_in, axis=-1, keepdims=True)
    grad_norm = grad_in * res_scale - residual * (res_scale * res_scale * res_scale * dot_mean)
    grg[e] = (cot_own + grad_norm).astype(BF)

    gr_sems = (ssem.at[8], sem_gr)
    out_sems = (ssem.at[9], sem_out)
    gather_z(grg, *gr_sems)
    gather_y(grg, *gr_sems)
    outg[e] = (residual + sums[0]).astype(BF)
    gather_next(grg, *gr_sems)
    gather_z(outg, *out_sems)
    gather_done(grg, sem_gr)

    for b in range(4):
        grmat[32 * b : 32 * b + 32, :] = (
            grg[4 * b : 4 * b + 4].astype(F32).reshape(32, D).astype(BF)
        )
    for b in range(8):
        pair = dot(head_t, grmat[:, b * 256 : (b + 1) * 256]).astype(BF)
        go_part[2 * b] = pair[:, :128]
        go_part[2 * b + 1] = pair[:, 128:]
    sum_start(go_part, go_near, ssem.at[10], sem_g1, 4, x, (0, 1))
    gather_y(outg, *out_sems)
    gather_next(outg, *out_sems)
    grad_att = dot_nt(grmat[...], wout[...]).astype(BF)
    soft_b = probs32[...]
    grad_probs = dot_nt(grad_att, v_act).astype(BF).astype(F32)
    grad_v = dot(probs_t, grad_att).astype(BF)
    sum_next(
        go_part, go_near, go_both, go_ring, ssem.at[11], sem_g1, sem_g2, 4, x, x_peer, (0, 1)
    )
    row_sum = jnp.sum(grad_probs * soft_b, axis=-1, keepdims=True)
    grad_scores = soft_b * (grad_probs - row_sum)
    grad_q = (dot(grad_scores.astype(BF), k_act) * FACTOR).astype(BF)
    grad_k = (dot(grad_scores.T.astype(BF), q_act) * FACTOR).astype(BF)
    stacked = (grad_q, grad_k, grad_v)
    for j in range(16):
        row = 384 * j
        while row < 384 * (j + 1):
            upto_row = min(384 * (j + 1), (row // D + 1) * D)
            f0 = row % D
            gq_part[j, row - 384 * j : upto_row - 384 * j, :] = dot(
                norm_t[f0 : f0 + upto_row - row, :], stacked[row // D]
            ).astype(BF)
            row = upto_row
    sum_start(gq_part, gq_near, ssem.at[15], sem_q1, 4, x, (0, 1))

    def sum_far(ring, far_out, far_in, s_sem, ring_sem, far_sem, z):
        far_out[z] = ring_sum(ring, ring_sem, 4, x, z).astype(BF)
        send(far_out.at[z], far_in.at[z], s_sem, far_sem.at[z], zsame)

    for z in range(2):
        sum_far(go_ring, go_out, go_in, ssem.at[12], sem_g2, sem_g3, z)
    sum_next(
        gq_part, gq_near, gq_both, gq_ring, ssem.at[16], sem_q1, sem_q2, 4, x, x_peer, (0, 1)
    )

    def fin_send(fin, slot, s_sem, r_sem, dev):
        send(fin.at[slot], fin.at[slot], s_sem, r_sem.at[slot], dev)

    def fin_first(far_out, far_in, fin, s_sem, r_sem, far_sem, z):
        seg = (c * 2 + z) * 4 + x
        arrived(far_in.at[z], far_sem.at[z])
        fin[seg] = (far_out[z].astype(F32) + far_in[z].astype(F32)).astype(BF)
        loop(1, 4, lambda k: fin_send(fin, seg, s_sem, r_sem, x_peer(k)[1]))
        fin_send(fin, seg, s_sem, r_sem, sib)

    def fin_last(fin, s_sem, r_sem, z):
        def step(k):
            slot = (c * 2 + z) * 4 + (x + 4 - k) % 4
            arrived(fin.at[slot], r_sem.at[slot])
            fin_send(fin, slot, s_sem, r_sem, sib)

        loop(1, 4, step)

    def fin_done(fin, r_sem):
        def step(k):
            slot = (1 - c) * 8 + k
            arrived(fin.at[slot], r_sem.at[slot])

        loop(0, 8, step)

    go_sems = (ssem.at[13], sem_go)
    gq_sems = (ssem.at[18], sem_gq)
    for z in range(2):
        fin_first(go_out, go_in, go_fin, *go_sems, sem_g3, z)
    for z in range(2):
        sum_far(gq_ring, gq_out, gq_in, ssem.at[17], sem_q2, sem_q3, z)
    for z in range(2):
        fin_first(gq_out, gq_in, gq_fin, *gq_sems, sem_q3, z)

    gather_done(outg, sem_out)
    row8 = lax.broadcasted_iota(jnp.int32, (8, 64), 0) + e * 8
    col8 = lax.broadcasted_iota(jnp.int32, (8, 64), 1)
    back_hot = jnp.zeros((8, 128), F32)
    for s in range(2):
        back_hot += dot_nt(jnp.where(row8 == col8 + 64 * s, 1.0, 0.0).astype(BF), place_hot[s])
    out_rows = outg[...].astype(F32).reshape(128, D).astype(BF)
    out_ref[...] = dot(back_hot.astype(BF), out_rows).astype(BF)

    for z in range(2):
        fin_last(go_fin, *go_sems, z)
    for z in range(2):
        fin_last(gq_fin, *gq_sems, z)
    fin_done(go_fin, sem_go)
    fin_done(gq_fin, sem_gq)

    sent(gath.at[pl.ds(0, 15)], ssem.at[0])
    sent(cotg.at[pl.ds(0, 15)], ssem.at[1])
    sent(party.at[pl.ds(0, 3)], ssem.at[2])
    sent(partz, ssem.at[14])
    sent(cotr.at[pl.ds(0, 31)], ssem.at[3])
    sent(tokg.at[pl.ds(0, 31)], ssem.at[4])
    sent(r1, ssem.at[5])
    sent(r2.at[pl.ds(0, 14)], ssem.at[6])
    sent(r3, ssem.at[7])
    sent(grg.at[pl.ds(0, 15)], ssem.at[8])
    sent(outg.at[pl.ds(0, 15)], ssem.at[9])
    sent(go_near, ssem.at[10])
    sent(go_ring.at[pl.ds(0, 6)], ssem.at[11])
    sent(go_in, ssem.at[12])
    sent(go_fin.at[pl.ds(0, 14)], ssem.at[13])
    sent(gq_near, ssem.at[15])
    sent(gq_ring.at[pl.ds(0, 6)], ssem.at[16])
    sent(gq_in, ssem.at[17])
    sent(gq_fin.at[pl.ds(0, 14)], ssem.at[18])


def layer(patches, visible, modality, dropped, again, w_qkv, w_out, fgain, wg, wu, wd, cot):
    vm = pl.BlockSpec(memory_space=pltpu.VMEM)
    anywhere = pl.BlockSpec(memory_space=pl.ANY)
    dma = pltpu.SemaphoreType.DMA
    scratch = [
        pltpu.VMEM((3, D, 128), BF),
        pltpu.VMEM((128, D), BF),
        pltpu.VMEM((D, 256), BF),
        pltpu.VMEM((D, 256), BF),
        pltpu.VMEM((256, D), BF),
        pltpu.VMEM((16, 16, 8, 128), BF),
        pltpu.VMEM((16, 8, D), BF),
        pltpu.VMEM((4, 4, 8, D), BF),
        pltpu.VMEM((4, 4, 8, D), BF),
        pltpu.VMEM((4, 8, D), BF),
        pltpu.VMEM((3, 8, D), BF),
        pltpu.VMEM((128, D), BF),
        pltpu.VMEM((D, 128), BF),
        pltpu.VMEM((128, 128), F32),
        pltpu.VMEM((32, 8, D), BF),
        pltpu.VMEM((32, 8, D), BF),
        pltpu.VMEM((256, D), BF),
        pltpu.VMEM((256, D), BF),
        pltpu.VMEM((32, 2, 8, D), BF),
        pltpu.VMEM((16, 2, 8, D), BF),
        pltpu.VMEM((16, 2, 8, D), BF),
        pltpu.VMEM((16, 2, 8, D), BF),
        pltpu.VMEM((2, 8, D), BF),
        pltpu.VMEM((2, 8, D), BF),
        pltpu.VMEM((16, 8, D), BF),
        pltpu.VMEM((16, 8, D), BF),
        pltpu.VMEM((128, D), BF),
        pltpu.VMEM((16, 128, 128), BF),
        pltpu.VMEM((8, 128, 128), BF),
        pltpu.VMEM((8, 128, 128), BF),
        pltpu.VMEM((8, 128, 128), BF),
        pltpu.VMEM((2, 128, 128), BF),
        pltpu.VMEM((2, 128, 128), BF),
        pltpu.VMEM((16, 384, 128), BF),
        pltpu.VMEM((8, 384, 128), BF),
        pltpu.VMEM((8, 384, 128), BF),
        pltpu.VMEM((8, 384, 128), BF),
        pltpu.VMEM((2, 384, 128), BF),
        pltpu.VMEM((2, 384, 128), BF),
        dma((5,)),
        dma((19,)),
        dma((16,)),
        dma((16,)),
        dma((4,)),
        dma((3,)),
        dma((32,)),
        dma((32,)),
        dma((16,)),
        dma((16,)),
        dma((1,)),
        dma((16,)),
        dma((16,)),
        dma((8,)),
        dma((8,)),
        dma((2,)),
        dma((16,)),
        dma((8,)),
        dma((8,)),
        dma((2,)),
        dma((16,)),
    ]
    out, gq, go = pl.pallas_call(
        kernel,
        out_shape=(
            jax.ShapeDtypeStruct((8, D), BF),
            jax.ShapeDtypeStruct((16, 384, 128), BF),
            jax.ShapeDtypeStruct((16, 128, 128), BF),
        ),
        in_specs=[pl.BlockSpec(memory_space=pltpu.SMEM)] + [vm] * 6 + [anywhere] * 5,
        out_specs=(vm, vm, vm),
        scratch_shapes=scratch,
        compiler_params=pltpu.CompilerParams(
            collective_id=0, has_side_effects=True, vmem_limit_bytes=56 * 1024 * 1024
        ),
        name="layer",
    )(
        dropped,
        patches,
        visible,
        modality,
        again.reshape(16, 128),
        fgain.reshape(1, D),
        cot,
        w_qkv.transpose(1, 0, 2),
        w_out,
        wg[0],
        wu[0],
        wd[0],
    )
    grad_qkv = gq.reshape(3, D, 128).transpose(1, 0, 2).astype(F32)
    grad_out = go.transpose(1, 0, 2).reshape(128, D).astype(F32)
    return out, grad_qkv, grad_out


def solution(mesh):
    placed = (
        P("dp", None, "expert"),
        P("dp", None),
        P("dp", None),
        P("dp"),
        P(),
        P(None, None, "expert"),
        P("expert", None),
        P(),
        P("expert", None, "dp"),
        P("expert", None, "dp"),
        P("expert", "dp", None),
        P(("dp", "expert"), None),
    )
    return jax.shard_map(
        layer,
        mesh=mesh,
        in_specs=placed,
        out_specs=(P(("dp", "expert"), None), P(None, None, "expert"), P("expert", None)),
        check_vma=False,
    )
```

```python
import math

import jax
import jax.numpy as jnp
from jax import lax
from jax.experimental import pallas as pl
from jax.experimental.pallas import tpu as pltpu
from jax.sharding import PartitionSpec as P

BF = jnp.bfloat16
F32 = jnp.float32
MESH = pl.DeviceIdType.MESH
D = 2048
EPS = 1e-06
FACTOR = 1.0 / math.sqrt(128)


def dot(a, b):
    return jnp.dot(a, b, preferred_element_type=F32)


def dot_nt(a, b):
    return lax.dot_general(a, b, (((1,), (1,)), ((), ())), preferred_element_type=F32)


def kernel(
    dropped_ref,
    patches_ref,
    visible_ref,
    modality_ref,
    again_ref,
    fgain_ref,
    cot_ref,
    wqkv_hbm,
    wout_hbm,
    wg_hbm,
    wu_hbm,
    wd_hbm,
    out_ref,
    gq_fin,
    go_ref,
    wqkv,
    wout,
    wg,
    wu,
    wd,
    gath,
    cotg,
    part,
    party,
    zsum,
    partz,
    normed,
    norm_t,
    probs32,
    tokg,
    cotr,
    tmat,
    cmat,
    osum,
    r1,
    s1,
    r2,
    s3,
    r3,
    outg,
    grg,
    grmat,
    go_part,
    go_near,
    go_both,
    go_ring,
    go_out,
    go_in,
    go_fin,
    gq_part,
    gq_near,
    gq_both,
    gq_ring,
    gq_out,
    gq_in,
    wsem,
    ssem,
    sem_pick,
    sem_cot,
    sem_ay,
    sem_az,
    sem_tok,
    sem_cotr,
    sem_d1,
    sem_d2,
    sem_d3,
    sem_gr,
    sem_out,
    sem_g1,
    sem_g2,
    sem_g3,
    sem_go,
    sem_q1,
    sem_q2,
    sem_q3,
    sem_gq,
):
    d = lax.axis_index("dp")
    e = lax.axis_index("expert")
    zh = d // 8
    x = (d // 2) % 4
    c = d % 2
    zl = e // 4
    y = e % 4
    h = y % 2
    xh = x * 2 + h
    sib = (zh * 8 + x * 2 + (1 - c), e)
    z_row = (1 - zh) * 8 + x * 2 + c
    zpart = (z_row, ((6 - zl) % 4) * 4 + y)
    zsame = (z_row, e)

    def z_peer(k):
        q = (zl + k) % 4
        return q, (d, q * 4 + y)

    def y_peer(k):
        q = (y + k) % 4
        return q, (d, zl * 4 + q)

    def xh_peer(k):
        q = (xh + k) % 8
        return q, (zh * 8 + (q // 2) * 2 + c, zl * 4 + (y // 2) * 2 + q % 2)

    def x_peer(k):
        q = (x + k) % 4
        return q, (zh * 8 + q * 2 + c, e)

    def send(src, dst, s_sem, r_sem, dev):
        pltpu.make_async_remote_copy(
            src_ref=src, dst_ref=dst, send_sem=s_sem, recv_sem=r_sem,
            device_id=dev, device_id_type=MESH,
        ).start()

    def arrived(dst, r_sem):
        pltpu.make_async_remote_copy(
            src_ref=dst, dst_ref=dst, send_sem=ssem.at[0], recv_sem=r_sem,
            device_id=sib, device_id_type=MESH,
        ).wait_recv()

    def sent(src, s_sem):
        pltpu.make_async_remote_copy(
            src_ref=src, dst_ref=src, send_sem=s_sem, recv_sem=sem_d3.at[0],
            device_id=sib, device_id_type=MESH,
        ).wait_send()

    def loop(lo, hi, fn):
        def step(k, carry):
            fn(k)
            return carry

        lax.fori_loop(lo, hi, step, 0)

    def gather_z(buf, s_sem, r_sem):
        loop(1, 4, lambda k: send(buf.at[e], buf.at[e], s_sem, r_sem.at[e], z_peer(k)[1]))

    def gather_y(buf, s_sem, r_sem):
        loop(1, 4, lambda k: send(buf.at[e], buf.at[e], s_sem, r_sem.at[e], y_peer(k)[1]))

    def gather_next(buf, s_sem, r_sem):
        def step(j):
            slot = ((zl + 4 - j) % 4) * 4 + y
            arrived(buf.at[slot], r_sem.at[slot])
            loop(
                1, 4,
                lambda k: send(buf.at[slot], buf.at[slot], s_sem, r_sem.at[slot], y_peer(k)[1]),
            )

        loop(1, 4, step)

    def gather_done(buf, r_sem):
        def step(j):
            def inner(k):
                slot = ((zl + 4 - j) % 4) * 4 + (y + 4 - k) % 4
                arrived(buf.at[slot], r_sem.at[slot])

            loop(1, 4, inner)

        loop(0, 4, step)

    loads = [
        pltpu.make_async_copy(src, dst, wsem.at[i])
        for i, (src, dst) in enumerate(
            ((wqkv_hbm, wqkv), (wout_hbm, wout), (wg_hbm, wg), (wu_hbm, wu), (wd_hbm, wd))
        )
    ]
    for load in loads:
        load.start()

    barrier = pltpu.get_barrier_semaphore()

    def greet(dev):
        pl.semaphore_signal(barrier, inc=1, device_id=dev, device_id_type=MESH)

    loop(1, 4, lambda k: greet(z_peer(k)[1]))
    loop(1, 4, lambda k: greet(y_peer(k)[1]))
    loop(1, 8, lambda k: greet(xh_peer(k)[1]))
    greet(sib)
    greet(zpart)
    greet(zsame)

    mod = modality_ref[...].astype(F32)
    upto = (
        lax.broadcasted_iota(jnp.int32, (64, 64), 0) <= lax.broadcasted_iota(jnp.int32, (64, 64), 1)
    ).astype(F32)
    samp_col = lax.broadcasted_iota(jnp.int32, (2, 64), 0).astype(F32)
    rank_sar = dot(mod, upto) - 1.0
    rank_opt = dot(1.0 - mod, upto) - 1.0
    place = jnp.where(mod > 0.5, 96.0 + 16.0 * samp_col + rank_sar, 48.0 * samp_col + rank_opt)
    slot_iota = lax.broadcasted_iota(jnp.int32, (128, 64), 0).astype(F32)
    patch_iota = lax.broadcasted_iota(jnp.int32, (256, 64), 0)
    place_hot = [
        jnp.where(slot_iota == place[s : s + 1, :], 1.0, 0.0).astype(BF) for s in range(2)
    ]
    picked = jnp.zeros((128, 128), F32)
    for s in range(2):
        patch_hot = jnp.where(patch_iota == visible_ref[s : s + 1, :], 1.0, 0.0).astype(BF)
        picked += dot(dot_nt(place_hot[s], patch_hot).astype(BF), patches_ref[s])
    gath[e] = picked.reshape(16, 8, 128).astype(BF)
    cotg[e] = cot_ref[...]

    pl.semaphore_wait(barrier, 16)

    pick_sems = (ssem.at[0], sem_pick)
    cot_sems = (ssem.at[1], sem_cot)
    gather_z(gath, *pick_sems)
    gather_y(gath, *pick_sems)
    gather_next(gath, *pick_sems)
    gather_z(cotg, *cot_sems)
    gather_y(cotg, *cot_sems)
    gather_next(cotg, *cot_sems)
    gather_done(gath, sem_pick)

    total = jnp.zeros((128, 128), F32)
    for b in range(16):
        xb = gath[b].astype(F32).reshape(128, 128)
        total += xb * xb
    scale = lax.rsqrt(jnp.sum(total, axis=-1, keepdims=True) * (1.0 / D) + EPS)
    for b in range(16):
        xb = gath[b].astype(F32).reshape(128, 128)
        normed[:, b * 128 : (b + 1) * 128] = (xb * scale * again_ref[b : b + 1, :]).astype(BF)
    loads[0].wait()
    q_act, k_act, v_act = (dot(normed[...], wqkv[i]).astype(BF) for i in range(3))
    row_i = lax.broadcasted_iota(jnp.int32, (128, 128), 0)
    col_i = lax.broadcasted_iota(jnp.int32, (128, 128), 1)

    def sample_of(i):
        second = jnp.logical_or(jnp.logical_and(i >= 48, i < 96), i >= 112)
        return jnp.where(second, 1, 0)

    drop0 = dropped_ref[0]
    drop1 = dropped_ref[1]
    col_samp = sample_of(col_i)
    col_drop = jnp.where(col_samp == 1, drop1, drop0)
    col_kind = jnp.where(col_i >= 96, 2, 1)
    keep = jnp.logical_and(sample_of(row_i) == col_samp, col_drop != col_kind)
    scores = jnp.where(keep, dot_nt(q_act, k_act) * FACTOR, -1e30)
    weights = jnp.exp(scores - jnp.max(scores, axis=-1, keepdims=True))
    soft = weights / jnp.sum(weights, axis=-1, keepdims=True)
    probs32[...] = soft
    head_out = dot(soft.astype(BF), v_act).astype(BF)
    loads[1].wait()
    for b in range(4):
        cols = slice(b * 512, (b + 1) * 512)
        rows = dot(head_out, wout[:, cols]).reshape(16, 8, 512).astype(BF)
        for i in range(16):
            part[i % 4, i // 4, :, cols] = rows[i]
    party[y] = part[y]

    def send_attn(k):
        q, dev = y_peer(k)
        send(part.at[q], party.at[y], ssem.at[2], sem_ay.at[y], dev)

    loop(1, 4, send_attn)

    own_slot = (c * 2 + zh) * 8 + xh

    def slot_of(core, q, z):
        return (core * 2 + z) * 8 + q

    gather_done(cotg, sem_cot)
    own_iota = (lax.broadcasted_iota(jnp.int32, (8, 64), 0) + e * 8).astype(F32)
    cot_own = jnp.zeros((8, D), F32)
    for s in range(2):
        hot = jnp.where(own_iota == place[s : s + 1, :], 1.0, 0.0).astype(BF)
        rows = cotg[8 * s : 8 * s + 8].astype(F32).reshape(64, D).astype(BF)
        cot_own += dot(hot, rows)
    cotr[own_slot] = cot_own.astype(BF)

    def spread_first(buf, s_sem, r_sem):
        src = buf.at[own_slot]
        send(src, src, s_sem, r_sem.at[own_slot], zpart)

        def step(k):
            send(src, src, s_sem, r_sem.at[own_slot], xh_peer(k)[1])

        loop(1, 8, step)
        send(src, src, s_sem, r_sem.at[own_slot], sib)

    def spread_next(buf, s_sem, r_sem):
        other = slot_of(c, xh, 1 - zh)
        src = buf.at[other]
        arrived(src, r_sem.at[other])

        def step(k):
            send(src, src, s_sem, r_sem.at[other], xh_peer(k)[1])

        loop(1, 8, step)
        send(src, src, s_sem, r_sem.at[other], sib)

    def spread_last(buf, s_sem, r_sem):
        for z in (zh, 1 - zh):

            def step(k):
                slot = slot_of(c, (xh + 8 - k) % 8, z)
                arrived(buf.at[slot], r_sem.at[slot])
                send(buf.at[slot], buf.at[slot], s_sem, r_sem.at[slot], sib)

            loop(1, 8, step)

    def spread_done(buf, r_sem):
        def step(k):
            slot = (1 - c) * 16 + k
            arrived(buf.at[slot], r_sem.at[slot])

        loop(0, 16, step)

    h_peer = (d, zl * 4 + y + 1 - 2 * h)

    def share(buf, slot, s_sem, r_sem, devs):
        src = buf.at[slot]
        for dev in devs:
            send(src, src, s_sem, r_sem.at[slot], dev)
        loop(1, 4, lambda k: send(src, src, s_sem, r_sem.at[slot], x_peer(k)[1]))

    share(cotr, own_slot, ssem.at[3], sem_cotr, (zpart, h_peer, sib))
    for b in range(16):
        cols = slice(b * 128, (b + 1) * 128)
        norm_t[cols, :] = normed[:, cols].astype(F32).T.astype(BF)
    head_t = head_out.astype(F32).T.astype(BF)
    probs_t = soft.T.astype(BF)

    def cot_pass(slot, devs):
        arrived(cotr.at[slot], sem_cotr.at[slot])
        share(cotr, slot, ssem.at[3], sem_cotr, devs)

    def cot_rest():
        for z in (zh, 1 - zh):
            for other in (0, 1):

                def step(k):
                    row = (x + 4 - k) % 4 * 2
                    slot = slot_of(c, row + (h if other == 0 else 1 - h), z)
                    arrived(cotr.at[slot], sem_cotr.at[slot])
                    send(cotr.at[slot], cotr.at[slot], ssem.at[3], sem_cotr.at[slot], sib)

                loop(1, 4, step)

    def wait_ay(k):
        q = (y + k) % 4
        arrived(party.at[q], sem_ay.at[q])

    loop(1, 4, wait_ay)

    def y_sum(z):
        acc = party[0, z].astype(F32)
        for b in range(1, 4):
            acc += party[b, z].astype(F32)
        return acc

    def send_az(k):
        q, dev = z_peer(k)
        zsum[q] = y_sum(q).astype(BF)
        send(zsum.at[q], partz.at[k - 1], ssem.at[14], sem_az.at[k - 1], dev)

    loop(1, 4, send_az)
    cot_pass(slot_of(c, xh, 1 - zh), (h_peer, sib))
    cot_pass(slot_of(c, x * 2 + 1 - h, zh), (sib,))
    cot_pass(slot_of(c, x * 2 + 1 - h, 1 - zh), (sib,))
    attn_sum = y_sum(zl)
    own = jnp.concatenate([gath[b, e].astype(F32) for b in range(16)], axis=-1)
    loop(0, 3, lambda k: arrived(partz.at[k], sem_az.at[k]))
    for b in range(3):
        attn_sum += partz[b].astype(F32)
    residual = own + attn_sum
    res_scale = lax.rsqrt(jnp.mean(residual * residual, axis=-1, keepdims=True) + EPS)
    fgain = fgain_ref[...]
    tokg[own_slot] = (residual * res_scale * fgain).astype(BF)
    spread_first(tokg, ssem.at[4], sem_tok)
    spread_next(tokg, ssem.at[4], sem_tok)
    cot_rest()
    spread_last(tokg, ssem.at[4], sem_tok)
    for i in (2, 3, 4):
        loads[i].wait()

    def pack_rows(dst, buf, core):
        for b in range(4):
            rows = buf[pl.ds(core * 16 + 4 * b, 4)].astype(F32).reshape(32, D)
            dst[core, 32 * b : 32 * b + 32, :] = rows.astype(BF)

    def experts(core):
        pack_rows(cmat, cotr, core)
        pack_rows(tmat, tokg, core)
        tok = tmat[core]
        grad_hidden = dot_nt(cmat[core], wd[...])
        gate = dot(tok, wg[...])
        up = dot(tok, wu[...])
        logistic = jax.nn.sigmoid(gate)
        active = gate * logistic
        hidden = (active * up).astype(BF)
        grad_gate = (grad_hidden * up * logistic * (1.0 + gate * (1.0 - logistic))).astype(BF)
        grad_up = (grad_hidden * active).astype(BF)
        slots = pl.ds(core * 16, 16)
        for b in range(4):
            cols = slice(b * 512, (b + 1) * 512)
            osum[slots, 0, :, cols] = dot(hidden, wd[:, cols]).reshape(16, 8, 512).astype(BF)
            back = dot_nt(grad_gate, wg[cols, :]) + dot_nt(grad_up, wu[cols, :])
            osum[slots, 1, :, cols] = back.reshape(16, 8, 512).astype(BF)

    experts(c)
    spread_done(cotr, sem_cotr)
    spread_done(tokg, sem_tok)
    experts(1 - c)

    def sum_start(buf, near, s_sem, r_sem, n, me, halves):
        for z in halves:

            def step(k):
                i = z * n + (me + k) % n
                send(buf.at[(1 - c) * 2 * n + i], near.at[i], s_sem, r_sem.at[i], sib)

            loop(1, n + 1, step)

    def sum_next(buf, near, both, ring, s_sem, near_sem, ring_sem, n, me, peer, halves):
        for z in halves:

            def add(q):
                i = z * n + q
                arrived(near.at[i], near_sem.at[i])
                return (buf[c * 2 * n + i].astype(F32) + near[i].astype(F32)).astype(BF)

            def step(k):
                q, dev = peer(k)
                i = z * n + q
                both[i] = add(q)
                send(both.at[i], ring.at[z * n + me], s_sem, ring_sem.at[z * n + me], dev)

            loop(1, n, step)
            ring[z * n + me] = add(me)

    def ring_sum(ring, ring_sem, n, me, z):
        def step(k):
            i = z * n + (me + k) % n
            arrived(ring.at[i], ring_sem.at[i])

        loop(1, n, step)
        acc = ring[z * n].astype(F32)
        for b in range(1, n):
            acc += ring[z * n + b].astype(F32)
        return acc

    sum_start(osum, r1, ssem.at[5], sem_d1, 8, xh, (1 - zh, zh))
    sum_next(osum, r1, s1, r2, ssem.at[6], sem_d1, sem_d2, 8, xh, xh_peer, (1 - zh, zh))
    s3[...] = ring_sum(r2, sem_d2, 8, xh, 1 - zh).astype(BF)
    send(s3, r3, ssem.at[7], sem_d3.at[0], zpart)
    sums = ring_sum(r2, sem_d2, 8, xh, zh)
    arrived(r3, sem_d3.at[0])
    own_second = jnp.where(
        jnp.logical_or(jnp.logical_and(e >= 6, e < 12), e >= 14), drop1, drop0
    )
    own_kind = jnp.where(e >= 12, 2, 1)
    alive = jnp.where(own_second != own_kind, 1.0, 0.0)
    sums = (sums + r3[...].astype(F32)) * alive
    grad_in = sums[1] * fgain
    dot_mean = jnp.mean(residual * grad_in, axis=-1, keepdims=True)
    grad_norm = grad_in * res_scale - residual * (res_scale * res_scale * res_scale * dot_mean)
    grg[e] = (cot_own + grad_norm).astype(BF)

    gr_sems = (ssem.at[8], sem_gr)
    out_sems = (ssem.at[9], sem_out)
    gather_z(grg, *gr_sems)
    gather_y(grg, *gr_sems)
    outg[e] = (residual + sums[0]).astype(BF)
    gather_next(grg, *gr_sems)
    gather_z(outg, *out_sems)
    gather_done(grg, sem_gr)

    for b in range(4):
        grmat[32 * b : 32 * b + 32, :] = (
            grg[4 * b : 4 * b + 4].astype(F32).reshape(32, D).astype(BF)
        )
    for b in range(8):
        pair = dot(head_t, grmat[:, b * 256 : (b + 1) * 256]).astype(BF)
        go_part[2 * b] = pair[:, :128]
        go_part[2 * b + 1] = pair[:, 128:]
    sum_start(go_part, go_near, ssem.at[10], sem_g1, 4, x, (0, 1))
    gather_y(outg, *out_sems)
    gather_next(outg, *out_sems)
    grad_att = dot_nt(grmat[...], wout[...]).astype(BF)
    soft_b = probs32[...]
    grad_probs = dot_nt(grad_att, v_act).astype(BF).astype(F32)
    grad_v = dot(probs_t, grad_att).astype(BF)
    sum_next(
        go_part, go_near, go_both, go_ring, ssem.at[11], sem_g1, sem_g2, 4, x, x_peer, (0, 1)
    )
    row_sum = jnp.sum(grad_probs * soft_b, axis=-1, keepdims=True)
    grad_scores = soft_b * (grad_probs - row_sum)
    grad_q = (dot(grad_scores.astype(BF), k_act) * FACTOR).astype(BF)
    grad_k = (dot(grad_scores.T.astype(BF), q_act) * FACTOR).astype(BF)
    stacked = (grad_q, grad_k, grad_v)
    for j in range(16):
        row = 384 * j
        while row < 384 * (j + 1):
            upto_row = min(384 * (j + 1), (row // D + 1) * D)
            f0 = row % D
            gq_part[j, row - 384 * j : upto_row - 384 * j, :] = dot(
                norm_t[f0 : f0 + upto_row - row, :], stacked[row // D]
            ).astype(BF)
            row = upto_row
    sum_start(gq_part, gq_near, ssem.at[15], sem_q1, 4, x, (0, 1))

    def sum_far(ring, far_out, far_in, s_sem, ring_sem, far_sem, z):
        far_out[z] = ring_sum(ring, ring_sem, 4, x, z).astype(BF)
        send(far_out.at[z], far_in.at[z], s_sem, far_sem.at[z], zsame)

    for z in range(2):
        sum_far(go_ring, go_out, go_in, ssem.at[12], sem_g2, sem_g3, z)
    sum_next(
        gq_part, gq_near, gq_both, gq_ring, ssem.at[16], sem_q1, sem_q2, 4, x, x_peer, (0, 1)
    )

    def fin_send(fin, slot, s_sem, r_sem, dev):
        send(fin.at[slot], fin.at[slot], s_sem, r_sem.at[slot], dev)

    def fin_first(far_out, far_in, fin, s_sem, r_sem, far_sem, z):
        seg = (c * 2 + z) * 4 + x
        arrived(far_in.at[z], far_sem.at[z])
        fin[seg] = (far_out[z].astype(F32) + far_in[z].astype(F32)).astype(BF)
        loop(1, 4, lambda k: fin_send(fin, seg, s_sem, r_sem, x_peer(k)[1]))
        fin_send(fin, seg, s_sem, r_sem, sib)

    def fin_last(fin, s_sem, r_sem, z):
        def step(k):
            slot = (c * 2 + z) * 4 + (x + 4 - k) % 4
            arrived(fin.at[slot], r_sem.at[slot])
            fin_send(fin, slot, s_sem, r_sem, sib)

        loop(1, 4, step)

    def fin_done(fin, r_sem):
        def step(k):
            slot = (1 - c) * 8 + k
            arrived(fin.at[slot], r_sem.at[slot])

        loop(0, 8, step)

    go_sems = (ssem.at[13], sem_go)
    gq_sems = (ssem.at[18], sem_gq)
    for z in range(2):
        fin_first(go_out, go_in, go_fin, *go_sems, sem_g3, z)
    for z in range(2):
        sum_far(gq_ring, gq_out, gq_in, ssem.at[17], sem_q2, sem_q3, z)
    for z in range(2):
        fin_first(gq_out, gq_in, gq_fin, *gq_sems, sem_q3, z)

    gather_done(outg, sem_out)
    row8 = lax.broadcasted_iota(jnp.int32, (8, 64), 0) + e * 8
    col8 = lax.broadcasted_iota(jnp.int32, (8, 64), 1)
    back_hot = jnp.zeros((8, 128), F32)
    for s in range(2):
        back_hot += dot_nt(jnp.where(row8 == col8 + 64 * s, 1.0, 0.0).astype(BF), place_hot[s])
    out_rows = outg[...].astype(F32).reshape(128, D).astype(BF)
    out_ref[...] = dot(back_hot.astype(BF), out_rows).astype(BF)

    for z in range(2):
        fin_last(go_fin, *go_sems, z)
    fin_last(gq_fin, *gq_sems, 0)
    fin_done(go_fin, sem_go)
    for b in range(16):
        go_ref[:, b * 128 : (b + 1) * 128] = go_fin[b]
    fin_last(gq_fin, *gq_sems, 1)
    fin_done(gq_fin, sem_gq)

    sent(gath.at[pl.ds(0, 15)], ssem.at[0])
    sent(cotg.at[pl.ds(0, 15)], ssem.at[1])
    sent(party.at[pl.ds(0, 3)], ssem.at[2])
    sent(partz, ssem.at[14])
    sent(cotr.at[pl.ds(0, 31)], ssem.at[3])
    sent(tokg.at[pl.ds(0, 31)], ssem.at[4])
    sent(r1, ssem.at[5])
    sent(r2.at[pl.ds(0, 14)], ssem.at[6])
    sent(r3, ssem.at[7])
    sent(grg.at[pl.ds(0, 15)], ssem.at[8])
    sent(outg.at[pl.ds(0, 15)], ssem.at[9])
    sent(go_near, ssem.at[10])
    sent(go_ring.at[pl.ds(0, 6)], ssem.at[11])
    sent(go_in, ssem.at[12])
    sent(go_fin.at[pl.ds(0, 14)], ssem.at[13])
    sent(gq_near, ssem.at[15])
    sent(gq_ring.at[pl.ds(0, 6)], ssem.at[16])
    sent(gq_in, ssem.at[17])
    sent(gq_fin.at[pl.ds(0, 14)], ssem.at[18])


def layer(patches, visible, modality, dropped, again, w_qkv, w_out, fgain, wg, wu, wd, cot):
    vm = pl.BlockSpec(memory_space=pltpu.VMEM)
    anywhere = pl.BlockSpec(memory_space=pl.ANY)
    dma = pltpu.SemaphoreType.DMA
    scratch = [
        pltpu.VMEM((3, D, 128), BF),
        pltpu.VMEM((128, D), BF),
        pltpu.VMEM((D, 256), BF),
        pltpu.VMEM((D, 256), BF),
        pltpu.VMEM((256, D), BF),
        pltpu.VMEM((16, 16, 8, 128), BF),
        pltpu.VMEM((16, 8, D), BF),
        pltpu.VMEM((4, 4, 8, D), BF),
        pltpu.VMEM((4, 4, 8, D), BF),
        pltpu.VMEM((4, 8, D), BF),
        pltpu.VMEM((3, 8, D), BF),
        pltpu.VMEM((128, D), BF),
        pltpu.VMEM((D, 128), BF),
        pltpu.VMEM((128, 128), F32),
        pltpu.VMEM((32, 8, D), BF),
        pltpu.VMEM((32, 8, D), BF),
        pltpu.VMEM((2, 128, D), BF),
        pltpu.VMEM((2, 128, D), BF),
        pltpu.VMEM((32, 2, 8, D), BF),
        pltpu.VMEM((16, 2, 8, D), BF),
        pltpu.VMEM((16, 2, 8, D), BF),
        pltpu.VMEM((16, 2, 8, D), BF),
        pltpu.VMEM((2, 8, D), BF),
        pltpu.VMEM((2, 8, D), BF),
        pltpu.VMEM((16, 8, D), BF),
        pltpu.VMEM((16, 8, D), BF),
        pltpu.VMEM((128, D), BF),
        pltpu.VMEM((16, 128, 128), BF),
        pltpu.VMEM((8, 128, 128), BF),
        pltpu.VMEM((8, 128, 128), BF),
        pltpu.VMEM((8, 128, 128), BF),
        pltpu.VMEM((2, 128, 128), BF),
        pltpu.VMEM((2, 128, 128), BF),
        pltpu.VMEM((16, 128, 128), BF),
        pltpu.VMEM((16, 384, 128), BF),
        pltpu.VMEM((8, 384, 128), BF),
        pltpu.VMEM((8, 384, 128), BF),
        pltpu.VMEM((8, 384, 128), BF),
        pltpu.VMEM((2, 384, 128), BF),
        pltpu.VMEM((2, 384, 128), BF),
        dma((5,)),
        dma((19,)),
        dma((16,)),
        dma((16,)),
        dma((4,)),
        dma((3,)),
        dma((32,)),
        dma((32,)),
        dma((16,)),
        dma((16,)),
        dma((1,)),
        dma((16,)),
        dma((16,)),
        dma((8,)),
        dma((8,)),
        dma((2,)),
        dma((16,)),
        dma((8,)),
        dma((8,)),
        dma((2,)),
        dma((16,)),
    ]
    out, gq, go = pl.pallas_call(
        kernel,
        out_shape=(
            jax.ShapeDtypeStruct((8, D), BF),
            jax.ShapeDtypeStruct((16, 384, 128), BF),
            jax.ShapeDtypeStruct((128, D), BF),
        ),
        in_specs=[pl.BlockSpec(memory_space=pltpu.SMEM)] + [vm] * 6 + [anywhere] * 5,
        out_specs=(vm, vm, vm),
        scratch_shapes=scratch,
        compiler_params=pltpu.CompilerParams(
            collective_id=0, has_side_effects=True, vmem_limit_bytes=56 * 1024 * 1024
        ),
        name="layer",
    )(
        dropped,
        patches,
        visible,
        modality,
        again.reshape(16, 128),
        fgain.reshape(1, D),
        cot,
        w_qkv.transpose(1, 0, 2),
        w_out,
        wg[0],
        wu[0],
        wd[0],
    )
    grad_qkv = gq.reshape(3, D, 128).transpose(1, 0, 2).astype(F32)
    grad_out = go.astype(F32)
    return out, grad_qkv, grad_out


def solution(mesh):
    placed = (
        P("dp", None, "expert"),
        P("dp", None),
        P("dp", None),
        P("dp"),
        P(),
        P(None, None, "expert"),
        P("expert", None),
        P(),
        P("expert", None, "dp"),
        P("expert", None, "dp"),
        P("expert", "dp", None),
        P(("dp", "expert"), None),
    )
    return jax.shard_map(
        layer,
        mesh=mesh,
        in_specs=placed,
        out_specs=(P(("dp", "expert"), None), P(None, None, "expert"), P("expert", None)),
        check_vma=False,
    )
```

```python
import math

import jax
import jax.numpy as jnp
from jax import lax
from jax.experimental import pallas as pl
from jax.experimental.pallas import tpu as pltpu
from jax.sharding import PartitionSpec as P

BF = jnp.bfloat16
F32 = jnp.float32
MESH = pl.DeviceIdType.MESH
D = 2048
EPS = 1e-06
FACTOR = 1.0 / math.sqrt(128)


def dot(a, b):
    return jnp.dot(a, b, preferred_element_type=F32)


def dot_nt(a, b):
    return lax.dot_general(a, b, (((1,), (1,)), ((), ())), preferred_element_type=F32)


def kernel(
    dropped_ref,
    patches_ref,
    visible_ref,
    modality_ref,
    again_ref,
    fgain_ref,
    cot_ref,
    wqkv_hbm,
    wout_hbm,
    wg_hbm,
    wu_hbm,
    wd_hbm,
    out_ref,
    gq_fin,
    go_ref,
    wqkv,
    wout,
    wg,
    wu,
    wd,
    gath,
    cotg,
    part,
    party,
    zsum,
    partz,
    normed,
    norm_t,
    probs32,
    tokg,
    cotr,
    tmat,
    cmat,
    osum,
    r1,
    s1,
    r2,
    s3,
    r3,
    outg,
    grg,
    grmat,
    go_part,
    go_near,
    go_both,
    go_ring,
    go_out,
    go_in,
    go_fin,
    gq_part,
    gq_near,
    gq_both,
    gq_ring,
    gq_out,
    gq_in,
    wsem,
    ssem,
    sem_pick,
    sem_cot,
    sem_ay,
    sem_az,
    sem_tok,
    sem_cotr,
    sem_d1,
    sem_d2,
    sem_d3,
    sem_gr,
    sem_out,
    sem_g1,
    sem_g2,
    sem_g3,
    sem_go,
    sem_q1,
    sem_q2,
    sem_q3,
    sem_gq,
):
    d = lax.axis_index("dp")
    e = lax.axis_index("expert")
    zh = d // 8
    x = (d // 2) % 4
    c = d % 2
    zl = e // 4
    y = e % 4
    h = y % 2
    xh = x * 2 + h
    sib = (zh * 8 + x * 2 + (1 - c), e)
    z_row = (1 - zh) * 8 + x * 2 + c
    zpart = (z_row, ((6 - zl) % 4) * 4 + y)
    zsame = (z_row, e)

    def z_peer(k):
        q = (zl + k) % 4
        return q, (d, q * 4 + y)

    def y_peer(k):
        q = (y + k) % 4
        return q, (d, zl * 4 + q)

    def xh_peer(k):
        q = (xh + k) % 8
        return q, (zh * 8 + (q // 2) * 2 + c, zl * 4 + (y // 2) * 2 + q % 2)

    def x_peer(k):
        q = (x + k) % 4
        return q, (zh * 8 + q * 2 + c, e)

    def send(src, dst, s_sem, r_sem, dev):
        pltpu.make_async_remote_copy(
            src_ref=src, dst_ref=dst, send_sem=s_sem, recv_sem=r_sem,
            device_id=dev, device_id_type=MESH,
        ).start()

    def arrived(dst, r_sem):
        pltpu.make_async_remote_copy(
            src_ref=dst, dst_ref=dst, send_sem=ssem.at[0], recv_sem=r_sem,
            device_id=sib, device_id_type=MESH,
        ).wait_recv()

    def sent(src, s_sem):
        pltpu.make_async_remote_copy(
            src_ref=src, dst_ref=src, send_sem=s_sem, recv_sem=sem_d3.at[0],
            device_id=sib, device_id_type=MESH,
        ).wait_send()

    def loop(lo, hi, fn):
        def step(k, carry):
            fn(k)
            return carry

        lax.fori_loop(lo, hi, step, 0)

    def gather_z(buf, s_sem, r_sem):
        loop(1, 4, lambda k: send(buf.at[e], buf.at[e], s_sem, r_sem.at[e], z_peer(k)[1]))

    def gather_y(buf, s_sem, r_sem):
        loop(1, 4, lambda k: send(buf.at[e], buf.at[e], s_sem, r_sem.at[e], y_peer(k)[1]))

    def gather_next(buf, s_sem, r_sem):
        def step(j):
            slot = ((zl + 4 - j) % 4) * 4 + y
            arrived(buf.at[slot], r_sem.at[slot])
            loop(
                1, 4,
                lambda k: send(buf.at[slot], buf.at[slot], s_sem, r_sem.at[slot], y_peer(k)[1]),
            )

        loop(1, 4, step)

    def gather_done(buf, r_sem):
        def step(j):
            def inner(k):
                slot = ((zl + 4 - j) % 4) * 4 + (y + 4 - k) % 4
                arrived(buf.at[slot], r_sem.at[slot])

            loop(1, 4, inner)

        loop(0, 4, step)

    loads = [
        pltpu.make_async_copy(src, dst, wsem.at[i])
        for i, (src, dst) in enumerate(
            ((wqkv_hbm, wqkv), (wout_hbm, wout), (wg_hbm, wg), (wu_hbm, wu), (wd_hbm, wd))
        )
    ]
    for load in loads:
        load.start()

    barrier = pltpu.get_barrier_semaphore()

    def greet(dev):
        pl.semaphore_signal(barrier, inc=1, device_id=dev, device_id_type=MESH)

    loop(1, 4, lambda k: greet(z_peer(k)[1]))
    loop(1, 4, lambda k: greet(y_peer(k)[1]))
    loop(1, 8, lambda k: greet(xh_peer(k)[1]))
    greet(sib)
    greet(zpart)
    greet(zsame)

    mod = modality_ref[...].astype(F32)
    upto = (
        lax.broadcasted_iota(jnp.int32, (64, 64), 0) <= lax.broadcasted_iota(jnp.int32, (64, 64), 1)
    ).astype(F32)
    samp_col = lax.broadcasted_iota(jnp.int32, (2, 64), 0).astype(F32)
    rank_sar = dot(mod, upto) - 1.0
    rank_opt = dot(1.0 - mod, upto) - 1.0
    place = jnp.where(mod > 0.5, 96.0 + 16.0 * samp_col + rank_sar, 48.0 * samp_col + rank_opt)
    slot_iota = lax.broadcasted_iota(jnp.int32, (128, 64), 0).astype(F32)
    patch_iota = lax.broadcasted_iota(jnp.int32, (256, 64), 0)
    place_hot = [
        jnp.where(slot_iota == place[s : s + 1, :], 1.0, 0.0).astype(BF) for s in range(2)
    ]
    picked = jnp.zeros((128, 128), F32)
    for s in range(2):
        patch_hot = jnp.where(patch_iota == visible_ref[s : s + 1, :], 1.0, 0.0).astype(BF)
        picked += dot(dot_nt(place_hot[s], patch_hot).astype(BF), patches_ref[s])
    gath[e] = picked.reshape(16, 8, 128).astype(BF)
    cotg[e] = cot_ref[...]

    pl.semaphore_wait(barrier, 16)

    pick_sems = (ssem.at[0], sem_pick)
    cot_sems = (ssem.at[1], sem_cot)
    gather_z(gath, *pick_sems)
    gather_y(gath, *pick_sems)
    gather_next(gath, *pick_sems)
    gather_z(cotg, *cot_sems)
    gather_y(cotg, *cot_sems)
    gather_next(cotg, *cot_sems)
    gather_done(gath, sem_pick)

    total = jnp.zeros((128, 128), F32)
    for b in range(16):
        xb = gath[b].astype(F32).reshape(128, 128)
        total += xb * xb
    scale = lax.rsqrt(jnp.sum(total, axis=-1, keepdims=True) * (1.0 / D) + EPS)
    for b in range(16):
        xb = gath[b].astype(F32).reshape(128, 128)
        normed[:, b * 128 : (b + 1) * 128] = (xb * scale * again_ref[b : b + 1, :]).astype(BF)
    loads[0].wait()
    q_act, k_act, v_act = (dot(normed[...], wqkv[i]).astype(BF) for i in range(3))
    row_i = lax.broadcasted_iota(jnp.int32, (128, 128), 0)
    col_i = lax.broadcasted_iota(jnp.int32, (128, 128), 1)

    def sample_of(i):
        second = jnp.logical_or(jnp.logical_and(i >= 48, i < 96), i >= 112)
        return jnp.where(second, 1, 0)

    drop0 = dropped_ref[0]
    drop1 = dropped_ref[1]
    col_samp = sample_of(col_i)
    col_drop = jnp.where(col_samp == 1, drop1, drop0)
    col_kind = jnp.where(col_i >= 96, 2, 1)
    keep = jnp.logical_and(sample_of(row_i) == col_samp, col_drop != col_kind)
    scores = jnp.where(keep, dot_nt(q_act, k_act) * FACTOR, -1e30)
    weights = jnp.exp(scores - jnp.max(scores, axis=-1, keepdims=True))
    soft = weights / jnp.sum(weights, axis=-1, keepdims=True)
    probs32[...] = soft
    head_out = dot(soft.astype(BF), v_act).astype(BF)
    loads[1].wait()
    for b in range(4):
        cols = slice(b * 512, (b + 1) * 512)
        rows = dot(head_out, wout[:, cols]).reshape(16, 8, 512).astype(BF)
        for i in range(16):
            part[i % 4, i // 4, :, cols] = rows[i]
    party[y] = part[y]

    def send_attn(k):
        q, dev = y_peer(k)
        send(part.at[q], party.at[y], ssem.at[2], sem_ay.at[y], dev)

    loop(1, 4, send_attn)

    own_slot = (c * 2 + zh) * 8 + xh

    def slot_of(core, q, z):
        return (core * 2 + z) * 8 + q

    gather_done(cotg, sem_cot)
    own_iota = (lax.broadcasted_iota(jnp.int32, (8, 64), 0) + e * 8).astype(F32)
    cot_own = jnp.zeros((8, D), F32)
    for s in range(2):
        hot = jnp.where(own_iota == place[s : s + 1, :], 1.0, 0.0).astype(BF)
        rows = cotg[8 * s : 8 * s + 8].astype(F32).reshape(64, D).astype(BF)
        cot_own += dot(hot, rows)
    cotr[own_slot] = cot_own.astype(BF)

    def spread_first(buf, s_sem, r_sem):
        src = buf.at[own_slot]
        send(src, src, s_sem, r_sem.at[own_slot], zpart)

        def step(k):
            send(src, src, s_sem, r_sem.at[own_slot], xh_peer(k)[1])

        loop(1, 8, step)
        send(src, src, s_sem, r_sem.at[own_slot], sib)

    def spread_next(buf, s_sem, r_sem):
        other = slot_of(c, xh, 1 - zh)
        src = buf.at[other]
        arrived(src, r_sem.at[other])

        def step(k):
            send(src, src, s_sem, r_sem.at[other], xh_peer(k)[1])

        loop(1, 8, step)
        send(src, src, s_sem, r_sem.at[other], sib)

    def spread_last(buf, s_sem, r_sem):
        for z in (zh, 1 - zh):

            def step(k):
                slot = slot_of(c, (xh + 8 - k) % 8, z)
                arrived(buf.at[slot], r_sem.at[slot])
                send(buf.at[slot], buf.at[slot], s_sem, r_sem.at[slot], sib)

            loop(1, 8, step)

    def spread_done(buf, r_sem):
        def step(k):
            slot = (1 - c) * 16 + k
            arrived(buf.at[slot], r_sem.at[slot])

        loop(0, 16, step)

    h_peer = (d, zl * 4 + y + 1 - 2 * h)

    def share(buf, slot, s_sem, r_sem, devs):
        src = buf.at[slot]
        for dev in devs:
            send(src, src, s_sem, r_sem.at[slot], dev)
        loop(1, 4, lambda k: send(src, src, s_sem, r_sem.at[slot], x_peer(k)[1]))

    share(cotr, own_slot, ssem.at[3], sem_cotr, (zpart, h_peer, sib))
    for b in range(16):
        cols = slice(b * 128, (b + 1) * 128)
        norm_t[cols, :] = normed[:, cols].astype(F32).T.astype(BF)
    head_t = head_out.astype(F32).T.astype(BF)
    probs_t = soft.T.astype(BF)

    def cot_pass(slot, devs):
        arrived(cotr.at[slot], sem_cotr.at[slot])
        share(cotr, slot, ssem.at[3], sem_cotr, devs)

    def cot_rest():
        for z in (zh, 1 - zh):
            for other in (0, 1):

                def step(k):
                    row = (x + 4 - k) % 4 * 2
                    slot = slot_of(c, row + (h if other == 0 else 1 - h), z)
                    arrived(cotr.at[slot], sem_cotr.at[slot])
                    send(cotr.at[slot], cotr.at[slot], ssem.at[3], sem_cotr.at[slot], sib)

                loop(1, 4, step)

    def wait_ay(k):
        q = (y + k) % 4
        arrived(party.at[q], sem_ay.at[q])

    loop(1, 4, wait_ay)

    def y_sum(z):
        acc = party[0, z].astype(F32)
        for b in range(1, 4):
            acc += party[b, z].astype(F32)
        return acc

    def send_az(k):
        q, dev = z_peer(k)
        zsum[q] = y_sum(q).astype(BF)
        send(zsum.at[q], partz.at[k - 1], ssem.at[14], sem_az.at[k - 1], dev)

    loop(1, 4, send_az)
    cot_pass(slot_of(c, xh, 1 - zh), (h_peer, sib))
    cot_pass(slot_of(c, x * 2 + 1 - h, zh), (sib,))
    cot_pass(slot_of(c, x * 2 + 1 - h, 1 - zh), (sib,))
    attn_sum = y_sum(zl)
    own = jnp.concatenate([gath[b, e].astype(F32) for b in range(16)], axis=-1)
    loop(0, 3, lambda k: arrived(partz.at[k], sem_az.at[k]))
    for b in range(3):
        attn_sum += partz[b].astype(F32)
    residual = own + attn_sum
    res_scale = lax.rsqrt(jnp.mean(residual * residual, axis=-1, keepdims=True) + EPS)
    fgain = fgain_ref[...]
    tokg[own_slot] = (residual * res_scale * fgain).astype(BF)
    spread_first(tokg, ssem.at[4], sem_tok)
    spread_next(tokg, ssem.at[4], sem_tok)
    cot_rest()
    spread_last(tokg, ssem.at[4], sem_tok)
    for i in (2, 3, 4):
        loads[i].wait()

    def pack_rows(dst, buf, core):
        for b in range(4):
            rows = buf[pl.ds(core * 16 + 4 * b, 4)].astype(F32).reshape(32, D)
            dst[core, 32 * b : 32 * b + 32, :] = rows.astype(BF)

    def experts(core):
        pack_rows(cmat, cotr, core)
        pack_rows(tmat, tokg, core)
        tok = tmat[core]
        grad_hidden = dot_nt(cmat[core], wd[...])
        gate = dot(tok, wg[...])
        up = dot(tok, wu[...])
        logistic = jax.nn.sigmoid(gate)
        active = gate * logistic
        hidden = (active * up).astype(BF)
        grad_gate = (grad_hidden * up * logistic * (1.0 + gate * (1.0 - logistic))).astype(BF)
        grad_up = (grad_hidden * active).astype(BF)
        slots = pl.ds(core * 16, 16)
        for b in range(4):
            cols = slice(b * 512, (b + 1) * 512)
            osum[slots, 0, :, cols] = dot(hidden, wd[:, cols]).reshape(16, 8, 512).astype(BF)
            back = dot_nt(grad_gate, wg[cols, :]) + dot_nt(grad_up, wu[cols, :])
            osum[slots, 1, :, cols] = back.reshape(16, 8, 512).astype(BF)

    experts(c)
    spread_done(cotr, sem_cotr)
    spread_done(tokg, sem_tok)
    experts(1 - c)

    def sum_start(buf, near, s_sem, r_sem, n, me, halves):
        for z in halves:

            def step(k):
                i = z * n + (me + k) % n
                send(buf.at[(1 - c) * 2 * n + i], near.at[i], s_sem, r_sem.at[i], sib)

            loop(1, n + 1, step)

    def sum_next(buf, near, both, ring, s_sem, near_sem, ring_sem, n, me, peer, halves):
        for z in halves:

            def add(q):
                i = z * n + q
                arrived(near.at[i], near_sem.at[i])
                return (buf[c * 2 * n + i].astype(F32) + near[i].astype(F32)).astype(BF)

            def step(k):
                q, dev = peer(k)
                i = z * n + q
                both[i] = add(q)
                send(both.at[i], ring.at[z * n + me], s_sem, ring_sem.at[z * n + me], dev)

            loop(1, n, step)
            ring[z * n + me] = add(me)

    def ring_sum(ring, ring_sem, n, me, z):
        def step(k):
            i = z * n + (me + k) % n
            arrived(ring.at[i], ring_sem.at[i])

        loop(1, n, step)
        acc = ring[z * n].astype(F32)
        for b in range(1, n):
            acc += ring[z * n + b].astype(F32)
        return acc

    sum_start(osum, r1, ssem.at[5], sem_d1, 8, xh, (1 - zh, zh))
    sum_next(osum, r1, s1, r2, ssem.at[6], sem_d1, sem_d2, 8, xh, xh_peer, (1 - zh, zh))
    s3[...] = ring_sum(r2, sem_d2, 8, xh, 1 - zh).astype(BF)
    send(s3, r3, ssem.at[7], sem_d3.at[0], zpart)
    sums = ring_sum(r2, sem_d2, 8, xh, zh)
    arrived(r3, sem_d3.at[0])
    own_second = jnp.where(
        jnp.logical_or(jnp.logical_and(e >= 6, e < 12), e >= 14), drop1, drop0
    )
    own_kind = jnp.where(e >= 12, 2, 1)
    alive = jnp.where(own_second != own_kind, 1.0, 0.0)
    sums = (sums + r3[...].astype(F32)) * alive
    grad_in = sums[1] * fgain
    dot_mean = jnp.mean(residual * grad_in, axis=-1, keepdims=True)
    grad_norm = grad_in * res_scale - residual * (res_scale * res_scale * res_scale * dot_mean)
    grg[e] = (cot_own + grad_norm).astype(BF)

    gr_sems = (ssem.at[8], sem_gr)
    out_sems = (ssem.at[9], sem_out)
    gather_z(grg, *gr_sems)
    gather_y(grg, *gr_sems)
    outg[e] = (residual + sums[0]).astype(BF)
    gather_next(grg, *gr_sems)
    gather_z(outg, *out_sems)
    gather_done(grg, sem_gr)

    for b in range(4):
        grmat[32 * b : 32 * b + 32, :] = (
            grg[4 * b : 4 * b + 4].astype(F32).reshape(32, D).astype(BF)
        )
    for b in range(8):
        pair = dot(head_t, grmat[:, b * 256 : (b + 1) * 256]).astype(BF)
        go_part[2 * b] = pair[:, :128]
        go_part[2 * b + 1] = pair[:, 128:]
    sum_start(go_part, go_near, ssem.at[10], sem_g1, 4, x, (0, 1))
    gather_y(outg, *out_sems)
    gather_next(outg, *out_sems)
    grad_att = dot_nt(grmat[...], wout[...]).astype(BF)
    soft_b = probs32[...]
    grad_probs = dot_nt(grad_att, v_act).astype(BF).astype(F32)
    grad_v = dot(probs_t, grad_att).astype(BF)
    sum_next(
        go_part, go_near, go_both, go_ring, ssem.at[11], sem_g1, sem_g2, 4, x, x_peer, (0, 1)
    )
    row_sum = jnp.sum(grad_probs * soft_b, axis=-1, keepdims=True)
    grad_scores = soft_b * (grad_probs - row_sum)
    grad_q = (dot(grad_scores.astype(BF), k_act) * FACTOR).astype(BF)
    grad_k = (dot(grad_scores.T.astype(BF), q_act) * FACTOR).astype(BF)
    stacked = (grad_q, grad_k, grad_v)
    for j in range(16):
        row = 384 * j
        while row < 384 * (j + 1):
            upto_row = min(384 * (j + 1), (row // D + 1) * D)
            f0 = row % D
            gq_part[j, row - 384 * j : upto_row - 384 * j, :] = dot(
                norm_t[f0 : f0 + upto_row - row, :], stacked[row // D]
            ).astype(BF)
            row = upto_row
    sum_start(gq_part, gq_near, ssem.at[15], sem_q1, 4, x, (0, 1))

    def sum_far(ring, far_out, far_in, s_sem, ring_sem, far_sem, z):
        far_out[z] = ring_sum(ring, ring_sem, 4, x, z).astype(BF)
        send(far_out.at[z], far_in.at[z], s_sem, far_sem.at[z], zsame)

    for z in range(2):
        sum_far(go_ring, go_out, go_in, ssem.at[12], sem_g2, sem_g3, z)
    sum_next(
        gq_part, gq_near, gq_both, gq_ring, ssem.at[16], sem_q1, sem_q2, 4, x, x_peer, (0, 1)
    )

    def fin_send(fin, slot, s_sem, r_sem, dev):
        send(fin.at[slot], fin.at[slot], s_sem, r_sem.at[slot], dev)

    def fin_first(far_out, far_in, fin, s_sem, r_sem, far_sem, z):
        seg = (c * 2 + z) * 4 + x
        arrived(far_in.at[z], far_sem.at[z])
        fin[seg] = (far_out[z].astype(F32) + far_in[z].astype(F32)).astype(BF)
        loop(1, 4, lambda k: fin_send(fin, seg, s_sem, r_sem, x_peer(k)[1]))
        fin_send(fin, seg, s_sem, r_sem, sib)

    def fin_last(fin, s_sem, r_sem, z):
        def step(k):
            slot = (c * 2 + z) * 4 + (x + 4 - k) % 4
            arrived(fin.at[slot], r_sem.at[slot])
            fin_send(fin, slot, s_sem, r_sem, sib)

        loop(1, 4, step)

    def fin_done(fin, r_sem):
        def step(k):
            slot = (1 - c) * 8 + k
            arrived(fin.at[slot], r_sem.at[slot])

        loop(0, 8, step)

    go_sems = (ssem.at[13], sem_go)
    gq_sems = (ssem.at[18], sem_gq)
    for z in range(2):
        fin_first(go_out, go_in, go_fin, *go_sems, sem_g3, z)
    gather_done(outg, sem_out)
    row8 = lax.broadcasted_iota(jnp.int32, (8, 64), 0) + e * 8
    col8 = lax.broadcasted_iota(jnp.int32, (8, 64), 1)
    back_hot = jnp.zeros((8, 128), F32)
    for s in range(2):
        back_hot += dot_nt(jnp.where(row8 == col8 + 64 * s, 1.0, 0.0).astype(BF), place_hot[s])
    out_rows = outg[...].astype(F32).reshape(128, D).astype(BF)
    out_ref[...] = dot(back_hot.astype(BF), out_rows).astype(BF)

    for z in range(2):
        sum_far(gq_ring, gq_out, gq_in, ssem.at[17], sem_q2, sem_q3, z)
    for z in range(2):
        fin_last(go_fin, *go_sems, z)
    fin_done(go_fin, sem_go)
    for b in range(16):
        go_ref[:, b * 128 : (b + 1) * 128] = go_fin[b]
    for z in range(2):
        fin_first(gq_out, gq_in, gq_fin, *gq_sems, sem_q3, z)

    fin_last(gq_fin, *gq_sems, 0)
    fin_last(gq_fin, *gq_sems, 1)
    fin_done(gq_fin, sem_gq)

    sent(gath.at[pl.ds(0, 15)], ssem.at[0])
    sent(cotg.at[pl.ds(0, 15)], ssem.at[1])
    sent(party.at[pl.ds(0, 3)], ssem.at[2])
    sent(partz, ssem.at[14])
    sent(cotr.at[pl.ds(0, 31)], ssem.at[3])
    sent(tokg.at[pl.ds(0, 31)], ssem.at[4])
    sent(r1, ssem.at[5])
    sent(r2.at[pl.ds(0, 14)], ssem.at[6])
    sent(r3, ssem.at[7])
    sent(grg.at[pl.ds(0, 15)], ssem.at[8])
    sent(outg.at[pl.ds(0, 15)], ssem.at[9])
    sent(go_near, ssem.at[10])
    sent(go_ring.at[pl.ds(0, 6)], ssem.at[11])
    sent(go_in, ssem.at[12])
    sent(go_fin.at[pl.ds(0, 14)], ssem.at[13])
    sent(gq_near, ssem.at[15])
    sent(gq_ring.at[pl.ds(0, 6)], ssem.at[16])
    sent(gq_in, ssem.at[17])
    sent(gq_fin.at[pl.ds(0, 14)], ssem.at[18])


def layer(patches, visible, modality, dropped, again, w_qkv, w_out, fgain, wg, wu, wd, cot):
    vm = pl.BlockSpec(memory_space=pltpu.VMEM)
    anywhere = pl.BlockSpec(memory_space=pl.ANY)
    dma = pltpu.SemaphoreType.DMA
    scratch = [
        pltpu.VMEM((3, D, 128), BF),
        pltpu.VMEM((128, D), BF),
        pltpu.VMEM((D, 256), BF),
        pltpu.VMEM((D, 256), BF),
        pltpu.VMEM((256, D), BF),
        pltpu.VMEM((16, 16, 8, 128), BF),
        pltpu.VMEM((16, 8, D), BF),
        pltpu.VMEM((4, 4, 8, D), BF),
        pltpu.VMEM((4, 4, 8, D), BF),
        pltpu.VMEM((4, 8, D), BF),
        pltpu.VMEM((3, 8, D), BF),
        pltpu.VMEM((128, D), BF),
        pltpu.VMEM((D, 128), BF),
        pltpu.VMEM((128, 128), F32),
        pltpu.VMEM((32, 8, D), BF),
        pltpu.VMEM((32, 8, D), BF),
        pltpu.VMEM((2, 128, D), BF),
        pltpu.VMEM((2, 128, D), BF),
        pltpu.VMEM((32, 2, 8, D), BF),
        pltpu.VMEM((16, 2, 8, D), BF),
        pltpu.VMEM((16, 2, 8, D), BF),
        pltpu.VMEM((16, 2, 8, D), BF),
        pltpu.VMEM((2, 8, D), BF),
        pltpu.VMEM((2, 8, D), BF),
        pltpu.VMEM((16, 8, D), BF),
        pltpu.VMEM((16, 8, D), BF),
        pltpu.VMEM((128, D), BF),
        pltpu.VMEM((16, 128, 128), BF),
        pltpu.VMEM((8, 128, 128), BF),
        pltpu.VMEM((8, 128, 128), BF),
        pltpu.VMEM((8, 128, 128), BF),
        pltpu.VMEM((2, 128, 128), BF),
        pltpu.VMEM((2, 128, 128), BF),
        pltpu.VMEM((16, 128, 128), BF),
        pltpu.VMEM((16, 384, 128), BF),
        pltpu.VMEM((8, 384, 128), BF),
        pltpu.VMEM((8, 384, 128), BF),
        pltpu.VMEM((8, 384, 128), BF),
        pltpu.VMEM((2, 384, 128), BF),
        pltpu.VMEM((2, 384, 128), BF),
        dma((5,)),
        dma((19,)),
        dma((16,)),
        dma((16,)),
        dma((4,)),
        dma((3,)),
        dma((32,)),
        dma((32,)),
        dma((16,)),
        dma((16,)),
        dma((1,)),
        dma((16,)),
        dma((16,)),
        dma((8,)),
        dma((8,)),
        dma((2,)),
        dma((16,)),
        dma((8,)),
        dma((8,)),
        dma((2,)),
        dma((16,)),
    ]
    out, gq, go = pl.pallas_call(
        kernel,
        out_shape=(
            jax.ShapeDtypeStruct((8, D), BF),
            jax.ShapeDtypeStruct((16, 384, 128), BF),
            jax.ShapeDtypeStruct((128, D), BF),
        ),
        in_specs=[pl.BlockSpec(memory_space=pltpu.SMEM)] + [vm] * 6 + [anywhere] * 5,
        out_specs=(vm, vm, vm),
        scratch_shapes=scratch,
        compiler_params=pltpu.CompilerParams(
            collective_id=0, has_side_effects=True, vmem_limit_bytes=56 * 1024 * 1024
        ),
        name="layer",
    )(
        dropped,
        patches,
        visible,
        modality,
        again.reshape(16, 128),
        fgain.reshape(1, D),
        cot,
        w_qkv.transpose(1, 0, 2),
        w_out,
        wg[0],
        wu[0],
        wd[0],
    )
    grad_qkv = gq.reshape(3, D, 128).transpose(1, 0, 2).astype(F32)
    grad_out = go.astype(F32)
    return out, grad_qkv, grad_out


def solution(mesh):
    placed = (
        P("dp", None, "expert"),
        P("dp", None),
        P("dp", None),
        P("dp"),
        P(),
        P(None, None, "expert"),
        P("expert", None),
        P(),
        P("expert", None, "dp"),
        P("expert", None, "dp"),
        P("expert", "dp", None),
        P(("dp", "expert"), None),
    )
    return jax.shard_map(
        layer,
        mesh=mesh,
        in_specs=placed,
        out_specs=(P(("dp", "expert"), None), P(None, None, "expert"), P("expert", None)),
        check_vma=False,
    )
```
